32 devices in a mesh: dp: 16 (over z, x, core), tensor: 2 (over y).
Axes of the slice: x: 2, y: 2, z: 4, core: 2. Of those that a mesh axis runs over, the one named last changes fastest.
Arguments:
- tokens: bfloat16 [16384, 1024], P(('dp', 'tensor')), may hold values from -6 to 6
- lengths: int32 [16, 6], P('dp'), may hold values from 0 to 512, as said below
- project_weight: bfloat16 [3, 1024, 1024], P(None, 'dp', 'tensor'), may hold values from -0.25 to 0.25
- project_bias: float32 [2, 1024], P(None, 'tensor'), may hold values from -3 to 3
- output_weight: bfloat16 [1024, 1024], P('tensor', 'dp'), may hold values from -0.5 to 0.5
- output_bias: float32 [1024], replicated, may hold values from -2 to 2
- first_gain: float32 [1024], replicated, may hold values from 0.1 to 1.9
- first_shift: float32 [1024], replicated, may hold values from -3 to 3
- expand_weight: bfloat16 [1024, 4096], P('dp', 'tensor'), may hold values from -0.1875 to 0.1875
- expand_bias: float32 [4096], P('tensor'), may hold values from -3 to 3
- shrink_weight: bfloat16 [4096, 1024], P('tensor', 'dp'), may hold values from -0.125 to 0.125
- shrink_bias: float32 [1024], replicated, may hold values from -2 to 2
- second_gain: float32 [1024], replicated, may hold values from 0.1 to 1.9
- second_shift: float32 [1024], replicated, may hold values from -3 to 3
- cotangent: bfloat16 [16384, 1024], P(('dp', 'tensor')), may hold values from -6 to 6
Outputs:
- layer_output: bfloat16 [16384, 1024], P(('dp', 'tensor'))
- grad_tokens: bfloat16 [16384, 1024], P(('dp', 'tensor'))
- grad_project_weight: float32 [3, 1024, 1024], P(None, 'dp', 'tensor')
- grad_project_bias: float32 [2, 1024], P(None, 'tensor')
- grad_output_weight: float32 [1024, 1024], P('tensor', 'dp')
- grad_output_bias: float32 [1024], replicated
- grad_first_gain: float32 [1024], replicated
- grad_first_shift: float32 [1024], replicated
- grad_expand_weight: float32 [1024, 4096], P('dp', 'tensor')
- grad_expand_bias: float32 [4096], P('tensor')
- grad_shrink_weight: float32 [4096, 1024], P('tensor', 'dp')
- grad_shrink_bias: float32 [1024], replicated
- grad_second_gain: float32 [1024], replicated
- grad_second_shift: float32 [1024], replicated
The draws below stay inside these ranges and needn't reach their ends.
Inputs may be any that keep to these rules, and one draw needn't show every extreme that they name: In each buffer the lengths sum to between 512 and 1024; one buffer is filled to exactly 1024 and begins with a sequence of 512. Zero lengths come only after the last nonzero one.
All inputs are finite; a program needn't handle non-finite values.
Results may differ from the reference program's by a relative error of at most 0.023.
Values may be sent and summed in bfloat16 or wider, within the bound.
No kernel may reach another device: no remote copies, remote signals or barrier semaphores. Data moves between devices by JAX's collectives and lax.ppermute only.
A program may use at most 192 MiB of HBM per device.

```python
import jax
import jax.numpy as jnp
from jax import lax

D = 1024
HEADS = 16
HEAD_DIM = 64
FF = 4096
TOK_DEV = 1024
SEQ_MAX = 512
BLOCK = 512
SEQS = 6
TOKENS = 16384
N_DP = 16


def draw_lengths(key, part):
    key = jax.random.fold_in(key, 7)
    first_key, second_key, third_key = jax.random.split(key, 3)
    wanted = jax.random.randint(first_key, (N_DP, SEQS), SEQ_MAX // 2, SEQ_MAX + 1, dtype=jnp.int32)
    capacity = jax.random.randint(second_key, (N_DP,), TOK_DEV // 2, TOK_DEV + 1, dtype=jnp.int32)
    fullest = jax.random.randint(third_key, (), 0, N_DP, dtype=jnp.int32)
    device_rows = jnp.arange(N_DP, dtype=jnp.int32)
    slot_cols = jnp.arange(SEQS, dtype=jnp.int32)
    chosen = (device_rows[:, None] == fullest) & (slot_cols[None, :] == 0)
    wanted = jnp.where(chosen, SEQ_MAX, wanted)
    capacity = jnp.where(device_rows == fullest, TOK_DEV, capacity)
    starts = jnp.cumsum(wanted, axis=1, dtype=jnp.int32) - wanted
    return jnp.clip(capacity[:, None] - starts, 0, wanted).astype(jnp.int32)


def levels(stream_key, shape, cuts, low, largest):
    factor_of = 1.0
    for axis_at, shards_of in cuts:
        heights = jax.random.uniform(jax.random.fold_in(jax.random.fold_in(stream_key, 6), axis_at), (shards_of,), jnp.float32, low / len(cuts), largest / len(cuts))
        factor_of = factor_of * jnp.repeat(jnp.exp(heights), shape[axis_at] // shards_of).reshape((-1,) + (1,) * (len(shape) - 1 - axis_at))
    return factor_of


def noise(stream_key, shape, deviation, bound, cuts=(), kind=jnp.bfloat16):
    level = levels(stream_key, shape, cuts, -0.22, 0.18) if cuts else 1.0
    values = jax.random.normal(stream_key, shape, jnp.float32) * deviation * level
    return jnp.minimum(jnp.maximum(values, -bound), bound).astype(kind)


def setup_inputs(seed: int = 0) -> dict:
    keys = jax.random.split(jax.random.key(seed), 16)
    return {
        "tokens": noise(keys[0], (TOKENS, D), 1.0, 6.0, ((0, 32),)),
        "lengths": draw_lengths(jax.random.fold_in(keys[15], 71), 0),
        "project_weight": noise(keys[2], (3, D, D), (D // 2) ** -0.5, 0.25, ((1, 16), (2, 2))),
        "project_bias": noise(keys[3], (2, D), 0.5, 3.0, ((1, 2),), jnp.float32),
        "output_weight": noise(keys[4], (D, D), (D // 8) ** -0.5, 0.5, ((0, 2), (1, 16))),
        "output_bias": noise(keys[5], (D,), 0.3, 2.0, (), jnp.float32),
        "first_gain": jnp.clip(1.0 + 0.18 * jax.random.normal(keys[6], (D,), jnp.float32), 0.1, 1.9),
        "first_shift": noise(keys[7], (D,), 0.5, 3.0, (), jnp.float32),
        "expand_weight": noise(keys[8], (D, FF), D ** -0.5, 0.1875, ((0, 16), (1, 2))),
        "expand_bias": noise(keys[9], (FF,), 0.5, 3.0, ((0, 2),), jnp.float32),
        "shrink_weight": noise(keys[10], (FF, D), (FF // 2) ** -0.5, 0.125, ((0, 2), (1, 16))),
        "shrink_bias": noise(keys[11], (D,), 0.3, 2.0, (), jnp.float32),
        "second_gain": jnp.clip(1.0 + 0.18 * jax.random.normal(keys[12], (D,), jnp.float32), 0.1, 1.9),
        "second_shift": noise(keys[13], (D,), 0.5, 3.0, (), jnp.float32),
        "cotangent": noise(keys[14], (TOKENS, D), 1.0, 6.0, ((0, 32),)),
    }


norm_eps = 1e-05
big_negative = -1e+30
highest = lax.Precision.HIGHEST

@jax.custom_vjp
def low(v):
    return lax.optimization_barrier(v.astype(jnp.bfloat16)).astype(jnp.float32)

@jax.custom_vjp
def low_back(v):
    return v

def low_keep(v):
    return (low(v), None)

def low_pass(kept, grad):
    return (grad,)

def back_keep(v):
    return (v, None)

def back_low(kept, grad):
    return (low(grad),)
low.defvjp(low_keep, low_pass)
low_back.defvjp(back_keep, back_low)

def layer_norm(rows, gain_vec, shift_vec):
    average = lax.optimization_barrier(jnp.mean(rows, axis=-1, keepdims=True))
    centered = rows - average
    variance = lax.optimization_barrier(jnp.mean(centered * centered, axis=-1, keepdims=True))
    return centered * lax.rsqrt(variance + norm_eps) * gain_vec + shift_vec

def segments_of(length_row):
    ends = jnp.cumsum(length_row, dtype=jnp.int32)
    positions = jnp.arange(TOK_DEV, dtype=jnp.int32)
    segment = lax.optimization_barrier(jnp.sum((positions[:, None] >= ends[None, :]).astype(jnp.int32), axis=1, dtype=jnp.int32))
    return (segment, positions < ends[-1])

def attend(queries, keys_all, values_all, segment):

    def one_block(index):
        begin_row = (index * BLOCK).astype(jnp.int32)
        query_block = lax.dynamic_slice_in_dim(queries, begin_row, BLOCK, 0)
        segment_block = lax.dynamic_slice_in_dim(segment, begin_row, BLOCK, 0)
        scores = jnp.einsum('qhd,khd->hqk', query_block, keys_all, precision=highest) * HEAD_DIM ** (-0.5)
        scores = low_back(scores)
        same = segment_block[:, None] == segment[None, :]
        masked = jnp.where(same[None], scores, big_negative)
        top_score = lax.optimization_barrier(jnp.max(masked, axis=-1, keepdims=True))
        weights = jnp.exp(masked - top_score)
        probs = low(weights / lax.optimization_barrier(jnp.sum(weights, axis=-1, keepdims=True)))
        return jnp.einsum('hqk,khd->qhd', probs, values_all, precision=highest)
    pieces = lax.map(jax.checkpoint(one_block), jnp.arange(TOK_DEV // BLOCK, dtype=jnp.int32))
    return pieces.reshape(TOK_DEV, D)

def layer_block(params, rows, length_row):
    project_weight, project_bias, output_weight, output_bias, first_gain, first_shift, expand_weight, expand_bias, shrink_weight, shrink_bias, second_gain, second_shift = params
    segment, valid = segments_of(length_row)
    projected = jnp.einsum('rd,cde->cre', rows, project_weight, precision=highest)
    bias_rows = jnp.stack([project_bias[0], jnp.zeros_like(project_bias[0]), project_bias[1]])
    projected = low(low_back(projected + bias_rows[:, None, :]))
    heads_view = projected.reshape(3, TOK_DEV, HEADS, HEAD_DIM)
    mixed = attend(heads_view[0], heads_view[1], heads_view[2], segment)
    mixed = low(low_back(mixed))
    attn = low_back(jnp.dot(mixed, output_weight, precision=highest) + output_bias)
    normed_one = layer_norm(rows + attn, first_gain, first_shift)
    upper = low_back(jnp.dot(low(normed_one), expand_weight, precision=highest) + expand_bias)
    active = low(jax.nn.gelu(upper, approximate=False))
    branch = low_back(jnp.dot(active, shrink_weight, precision=highest) + shrink_bias)
    result = layer_norm(normed_one + branch, second_gain, second_shift)
    return jnp.where(valid[:, None], result, 0.0)

def reference(tokens, lengths, project_weight, project_bias, output_weight, output_bias, first_gain, first_shift, expand_weight, expand_bias, shrink_weight, shrink_bias, second_gain, second_shift, cotangent):
    params = tuple((item.astype(jnp.float32) for item in (project_weight, project_bias, output_weight, output_bias, first_gain, first_shift, expand_weight, expand_bias, shrink_weight, shrink_bias, second_gain, second_shift)))
    rows = tokens.astype(jnp.float32).reshape(N_DP, TOK_DEV, D)

    def forward(params_in, rows_in):
        return lax.map(lambda item: layer_block(params_in, item[0], item[1]), (rows_in, lengths))
    result, pullback = jax.vjp(forward, params, rows)
    grads, grad_rows = pullback(cotangent.astype(jnp.float32).reshape(N_DP, TOK_DEV, D))
    return (result.reshape(TOKENS, D).astype(jnp.bfloat16), grad_rows.reshape(TOKENS, D).astype(jnp.bfloat16), grads[0], grads[1], grads[2], grads[3], grads[4], grads[5], grads[6], grads[7], grads[8], grads[9], grads[10], grads[11])
```

```python
from functools import partial

import jax
import jax.numpy as jnp
from jax import lax
from jax.sharding import PartitionSpec as P

HEAD_DIM = 64
BLOCK = 512
EPS = 1e-05
BIG_NEGATIVE = -1e30
ALL = ("dp", "tensor")
Z, X, C, Y = range(4)
F32 = jnp.float32
BF16 = jnp.bfloat16


def digit_sizes():
    rest = lax.axis_size("dp")
    core = 2 if rest % 2 == 0 else 1
    rest //= core
    across = 2 if rest % 2 == 0 else 1
    rest //= across
    return (rest, across, core, lax.axis_size("tensor"))


def my_digits(sizes):
    dp = lax.axis_index("dp")
    return (
        dp // (sizes[X] * sizes[C]),
        dp // sizes[C] % sizes[X],
        dp % sizes[C],
        lax.axis_index("tensor"),
    )


def hop(value, sizes, digit, step=1):
    pairs = []
    nz, nx, nc, ny = sizes
    for z in range(nz):
        for x in range(nx):
            for c in range(nc):
                for y in range(ny):
                    there = [z, x, c, y]
                    there[digit] = (there[digit] + step) % sizes[digit]
                    source = ((z * nx + x) * nc + c) * ny + y
                    target = ((there[0] * nx + there[1]) * nc + there[2]) * ny + there[3]
                    pairs.append((source, target))
    return lax.ppermute(value, ALL, pairs)


def ring(value, sizes, digit):
    pieces = [value]
    for _ in range(sizes[digit] - 1):
        pieces.append(hop(pieces[-1], sizes, digit))
    return pieces


def place(pieces, index, axis):
    count = len(pieces)
    if count == 1:
        return jnp.expand_dims(pieces[0], axis)
    shape = list(pieces[0].shape)
    shape.insert(axis, count)
    out = jnp.zeros(shape, pieces[0].dtype)
    for k, piece in enumerate(pieces):
        out = lax.dynamic_update_index_in_dim(out, piece, (index - k) % count, axis)
    return out


def pick(value, index, axis):
    return lax.dynamic_index_in_dim(value, index, axis, keepdims=False)


def ring_sum(value, sizes, digit, index, axis):
    count = sizes[digit]
    if count == 1:
        return jnp.squeeze(value, axis)
    moving = pick(value, (index - 1) % count, axis)
    for k in range(1, count):
        moving = hop(moving, sizes, digit) + pick(value, (index - 1 - k) % count, axis)
    return moving


def gather_xzc(shard, sizes, at):
    rows, width = shard.shape
    both = place(ring(shard, sizes, X), at[X], 0)
    deep = place(ring(both, sizes, Z), at[Z], 0)
    full = place(ring(deep, sizes, C), at[C], 2)
    return full.reshape(-1, width)


def gather_zxyc(shard, sizes, at, widths):
    deep = place(ring(shard, sizes, Z), at[Z], 0)
    across = ring(deep, sizes, X)
    halves = list(zip(*[ring(piece, sizes, Y) for piece in across]))
    out = []
    for half in halves:
        cored = list(zip(*[ring(piece, sizes, C) for piece in half]))
        mats = []
        begin = 0
        for width in widths:
            parts = [
                place([p[..., begin : begin + width] for p in by_x], at[X], 1) for by_x in cored
            ]
            mats.append(place(parts, at[C], 2).reshape(-1, width))
            begin += width
        out.append(mats)
    return out


def gather_yzxc(shard, sizes, at):
    width = shard.shape[-1]
    halves = jnp.stack(ring(shard, sizes, Y))
    deep = place(ring(halves, sizes, Z), at[Z], 1)
    cored = [ring(piece, sizes, C) for piece in ring(deep, sizes, X)]
    out = []
    for k in range(sizes[Y]):
        parts = [place([by_c[c][k] for by_c in cored], at[X], 1) for c in range(sizes[C])]
        out.append(place(parts, at[C], 2).reshape(-1, width))
    return out


def core_sum(value, sizes, at):
    return ring_sum(value, sizes, C, at[C], 2)


def scatter_czx(full, sizes, at):
    width = full.shape[-1]
    parts = core_sum(full.reshape(sizes[Z], sizes[X], sizes[C], -1, width), sizes, at)
    return ring_sum(ring_sum(parts, sizes, Z, at[Z], 0), sizes, X, at[X], 0)


def y_sum(halves, sizes):
    count = sizes[Y]
    total = halves[0]
    for k in range(1, count):
        total = total + hop(halves[k], sizes, Y, -k)
    return total


def scatter_cyxz(halves, sizes, at):
    width = halves[0].shape[-1]
    parts = [
        core_sum(h.reshape(sizes[Z], sizes[X], sizes[C], -1, width), sizes, at) for h in halves
    ]
    mine = y_sum(parts, sizes)
    return ring_sum(ring_sum(mine, sizes, X, at[X], 1), sizes, Z, at[Z], 0)


def scatter_cxzy(halves, sizes, at):
    width = halves[0].shape[-1]
    parts = [
        core_sum(h.reshape(sizes[Z], sizes[X], sizes[C], -1, width), sizes, at) for h in halves
    ]
    parts = jnp.stack([ring_sum(p, sizes, X, at[X], 1) for p in parts], axis=1)
    parts = ring_sum(parts, sizes, Z, at[Z], 0)
    return y_sum([parts[k] for k in range(sizes[Y])], sizes)


def norm_parts(rows):
    average = jnp.mean(rows, axis=-1, keepdims=True)
    centered = rows - average
    scale = lax.rsqrt(jnp.mean(centered * centered, axis=-1, keepdims=True) + EPS)
    return centered * scale, scale


def norm_back(grad, unit, scale, gain):
    inner = grad * gain
    return scale * (
        inner
        - jnp.mean(inner, axis=-1, keepdims=True)
        - unit * jnp.mean(inner * unit, axis=-1, keepdims=True)
    )


def gelu_both(upper):
    below = 0.5 * lax.erfc(upper * -(0.5**0.5))
    density = jnp.exp(-0.5 * upper * upper) * 0.3989422804014327
    return upper * below, below + upper * density


def dot(a, b, dims):
    return lax.dot_general(a, b, (dims, ((), ())), preferred_element_type=F32)


NN = ((1,), (0,))
NT = ((1,), (1,))
TN = ((0,), (0,))


def attention(query, key, value, segment):
    rows, width = query.shape
    heads = width // HEAD_DIM
    scale = HEAD_DIM ** (-0.5)
    query, key, value = (t.reshape(rows, heads, HEAD_DIM) for t in (query, key, value))

    def attend_block(index):
        begin = index * BLOCK
        query_block = lax.dynamic_slice_in_dim(query, begin, BLOCK, 0)
        segment_block = lax.dynamic_slice_in_dim(segment, begin, BLOCK, 0)
        scores = jnp.einsum("qhd,khd->hqk", query_block, key, preferred_element_type=F32) * scale
        same = segment_block[:, None] == segment[None, :]
        masked = jnp.where(same[None], scores, BIG_NEGATIVE)
        top = jnp.max(masked, axis=-1, keepdims=True)
        weights = jnp.exp(masked - top)
        totals = jnp.sum(weights, axis=-1, keepdims=True)
        low = (weights / totals).astype(BF16)
        mixed = jnp.einsum("hqk,khd->qhd", low, value, preferred_element_type=F32)
        return mixed.astype(BF16), top + jnp.log(totals)

    mixed, logs = lax.map(attend_block, jnp.arange(rows // BLOCK, dtype=jnp.int32))
    return mixed.reshape(rows, width), logs


def attention_back(query, key, value, segment, logs, grad):
    rows, width = query.shape
    heads = width // HEAD_DIM
    scale = HEAD_DIM ** (-0.5)
    query, key, value, grad = (
        t.reshape(rows, heads, HEAD_DIM) for t in (query, key, value, grad)
    )

    def attend_back(carry, index):
        key_grad, value_grad = carry
        begin = index * BLOCK
        query_block = lax.dynamic_slice_in_dim(query, begin, BLOCK, 0)
        segment_block = lax.dynamic_slice_in_dim(segment, begin, BLOCK, 0)
        grad_block = lax.dynamic_slice_in_dim(grad, begin, BLOCK, 0)
        scores = jnp.einsum("qhd,khd->hqk", query_block, key, preferred_element_type=F32) * scale
        same = segment_block[:, None] == segment[None, :]
        masked = jnp.where(same[None], scores, BIG_NEGATIVE)
        probs = jnp.exp(masked - logs[index])
        low = probs.astype(BF16)
        value_grad = value_grad + jnp.einsum(
            "hqk,qhd->khd", low, grad_block, preferred_element_type=F32
        )
        prob_grad = jnp.einsum("qhd,khd->hqk", grad_block, value, preferred_element_type=F32)
        inner = jnp.sum(probs * prob_grad, axis=-1, keepdims=True)
        score_grad = (probs * (prob_grad - inner)).astype(BF16)
        query_grad = (
            jnp.einsum("hqk,khd->qhd", score_grad, key, preferred_element_type=F32) * scale
        )
        key_grad = (
            key_grad
            + jnp.einsum("hqk,qhd->khd", score_grad, query_block, preferred_element_type=F32)
            * scale
        )
        return ((key_grad, value_grad), query_grad.astype(BF16))

    empty = jnp.zeros((rows, heads, HEAD_DIM), F32)
    (key_grad, value_grad), query_grad = lax.scan(
        attend_back, (empty, empty), jnp.arange(rows // BLOCK, dtype=jnp.int32)
    )
    return tuple(t.reshape(rows, width).astype(BF16) for t in (query_grad, key_grad, value_grad))


def on_device(
    tokens,
    lengths,
    project_weight,
    project_bias,
    output_weight,
    output_bias,
    first_gain,
    first_shift,
    expand_weight,
    expand_bias,
    shrink_weight,
    shrink_bias,
    second_gain,
    second_shift,
    cotangent,
):
    sizes = digit_sizes()
    at = my_digits(sizes)
    n_t = sizes[Y]
    mine = at[Y]
    rows, width = tokens.shape
    all_rows = rows * n_t
    heads_width = project_weight.shape[2]
    hidden = expand_weight.shape[1]
    depth = project_weight.shape[1]

    ends = jnp.cumsum(lengths[0], dtype=jnp.int32)
    positions = lax.iota(jnp.int32, all_rows)
    segment = jnp.sum(
        (positions[:, None] >= ends[None, :]).astype(jnp.int32), axis=1, dtype=jnp.int32
    )
    valid = (mine * rows + lax.iota(jnp.int32, rows) < ends[-1])[:, None]

    whole_tokens = place(ring(tokens, sizes, Y), mine, 0).reshape(all_rows, width)
    proj = gather_xzc(
        jnp.transpose(project_weight, (1, 0, 2)).reshape(depth, 3 * heads_width), sizes, at
    )
    gathered = gather_zxyc(
        jnp.concatenate([output_weight.T, expand_weight], axis=1),
        sizes,
        at,
        (heads_width, hidden),
    )
    mix = [g[0] for g in gathered]
    expand = [g[1] for g in gathered]
    shrink = gather_yzxc(shrink_weight.T, sizes, at)
    expand_biases = ring(expand_bias, sizes, Y)

    bias = jnp.concatenate([project_bias[0], jnp.zeros_like(project_bias[0]), project_bias[1]])
    projected = (dot(whole_tokens, proj, NN) + bias).astype(BF16)
    query, key, value = (
        projected[:, c * heads_width : (c + 1) * heads_width] for c in range(3)
    )
    mixed_heads, logs = attention(query, key, value, segment)
    by_rows = mixed_heads.reshape(n_t, rows, heads_width)
    mixed = [pick(by_rows, mine, 0)]
    for k in range(1, n_t):
        mixed.append(hop(pick(by_rows, (mine + k) % n_t, 0), sizes, Y, k))

    attn = sum(dot(m, w, NT) for m, w in zip(mixed, mix)) + output_bias
    unit1, scale1 = norm_parts(tokens.astype(F32) + attn)
    normed1 = unit1 * first_gain + first_shift
    low1 = normed1.astype(BF16)
    active, slope = [], []
    for w, b in zip(expand, expand_biases):
        act, der = gelu_both(dot(low1, w, NN) + b)
        active.append(act.astype(BF16))
        slope.append(der.astype(BF16))
    branch = sum(dot(a, w, NT) for a, w in zip(active, shrink)) + shrink_bias
    unit2, scale2 = norm_parts(normed1 + branch)
    layer_output = jnp.where(valid, unit2 * second_gain + second_shift, 0.0).astype(BF16)

    grad = jnp.where(valid, cotangent.astype(F32), 0.0)
    grad_second_gain = jnp.sum(grad * unit2, axis=0)
    grad_second_shift = jnp.sum(grad, axis=0)
    grad_r2 = norm_back(grad, unit2, scale2, second_gain)
    grad_branch = grad_r2.astype(BF16)
    grad_shrink_bias = jnp.sum(grad_branch, axis=0, dtype=F32)
    grad_shrink = [dot(grad_branch, a, TN).astype(BF16) for a in active]
    grad_shrink_weight = scatter_cxzy(grad_shrink, sizes, at).astype(F32).T
    grad_upper = [
        (dot(grad_branch, w, NN) * s.astype(F32)).astype(BF16) for w, s in zip(shrink, slope)
    ]
    grad_expand_biases = [jnp.sum(g, axis=0, dtype=F32) for g in grad_upper]
    grad_expand = [dot(low1, g, TN).astype(BF16) for g in grad_upper]
    grad_normed1 = sum(dot(g, w, NT) for g, w in zip(grad_upper, expand)) + grad_r2
    grad_first_gain = jnp.sum(grad_normed1 * unit1, axis=0)
    grad_first_shift = jnp.sum(grad_normed1, axis=0)
    grad_r1 = norm_back(grad_normed1, unit1, scale1, first_gain)
    grad_attn = grad_r1.astype(BF16)
    grad_output_bias = jnp.sum(grad_attn, axis=0, dtype=F32)

    grad_by_rows = jnp.zeros((n_t, rows, heads_width), BF16)
    for k, w in enumerate(mix):
        part = dot(grad_attn, w, NN).astype(BF16)
        if k:
            part = hop(part, sizes, Y, -k)
        grad_by_rows = lax.dynamic_update_index_in_dim(grad_by_rows, part, (mine + k) % n_t, 0)
    grad_mix = [dot(grad_attn, m, TN).astype(BF16) for m in mixed]
    owned = scatter_cyxz(
        [jnp.concatenate([a, b], axis=1) for a, b in zip(grad_mix, grad_expand)], sizes, at
    ).astype(F32)
    grad_output_weight = owned[:, :heads_width].T
    grad_expand_weight = owned[:, heads_width:]

    packed = jnp.concatenate(
        [
            grad_second_gain,
            grad_second_shift,
            grad_shrink_bias,
            grad_first_gain,
            grad_first_shift,
            grad_output_bias,
            place(grad_expand_biases, mine, 0).reshape(-1),
        ]
    )
    packed = lax.psum(packed, ALL)
    (
        grad_second_gain,
        grad_second_shift,
        grad_shrink_bias,
        grad_first_gain,
        grad_first_shift,
        grad_output_bias,
    ) = (packed[i * width : (i + 1) * width] for i in range(6))
    grad_expand_bias = pick(packed[6 * width :].reshape(n_t, hidden), mine, 0)

    projected_grad = jnp.concatenate(
        attention_back(
            query, key, value, segment, logs, grad_by_rows.reshape(all_rows, heads_width)
        ),
        axis=1,
    )
    grad_project_bias = lax.psum(
        jnp.stack(
            [
                jnp.sum(projected_grad[:, :heads_width], axis=0, dtype=F32),
                jnp.sum(projected_grad[:, 2 * heads_width :], axis=0, dtype=F32),
            ]
        ),
        "dp",
    )
    grad_project = scatter_czx(dot(whole_tokens, projected_grad, TN).astype(BF16), sizes, at)
    grad_project_weight = jnp.transpose(
        grad_project.reshape(depth, 3, heads_width), (1, 0, 2)
    ).astype(F32)
    token_grad = grad_r1
    for k in range(n_t):
        begin = (mine + k) % n_t * rows
        part = dot(lax.dynamic_slice_in_dim(projected_grad, begin, rows, 0), proj, NT)
        if k:
            part = hop(part.astype(BF16), sizes, Y, k).astype(F32)
        token_grad = token_grad + part
    grad_tokens = token_grad.astype(BF16)
    return (
        layer_output,
        grad_tokens,
        grad_project_weight,
        grad_project_bias,
        grad_output_weight,
        grad_output_bias,
        grad_first_gain,
        grad_first_shift,
        grad_expand_weight,
        grad_expand_bias,
        grad_shrink_weight,
        grad_shrink_bias,
        grad_second_gain,
        grad_second_shift,
    )


def solution(mesh):
    rows = P(("dp", "tensor"), None)
    weights = (P(None, "dp", "tensor"), P("tensor", "dp"), P("dp", "tensor"), P("tensor", "dp"))
    in_specs = (
        rows,
        P("dp", None),
        weights[0],
        P(None, "tensor"),
        weights[1],
        P(),
        P(),
        P(),
        weights[2],
        P("tensor"),
        weights[3],
        P(),
        P(),
        P(),
        rows,
    )
    out_specs = (
        rows,
        rows,
        weights[0],
        P(None, "tensor"),
        weights[1],
        P(),
        P(),
        P(),
        weights[2],
        P("tensor"),
        weights[3],
        P(),
        P(),
        P(),
    )
    return jax.shard_map(
        on_device, mesh=mesh, in_specs=in_specs, out_specs=out_specs, check_vma=False
    )
```

```python
import jax
import jax.numpy as jnp
from jax import lax
from jax.experimental import pallas as pl
from jax.experimental.pallas import tpu as pltpu
from jax.sharding import PartitionSpec as P

HEAD_DIM = 64
TILE = 256
PAIR = 2 * HEAD_DIM
EPS = 1e-05
BIG_NEGATIVE = -1e30
ALL = ("dp", "tensor")
Z, X, C, Y = range(4)
F32 = jnp.float32
BF16 = jnp.bfloat16


def digit_sizes():
    rest = lax.axis_size("dp")
    core = 2 if rest % 2 == 0 else 1
    rest //= core
    across = 2 if rest % 2 == 0 else 1
    rest //= across
    return (rest, across, core, lax.axis_size("tensor"))


def my_digits(sizes):
    dp = lax.axis_index("dp")
    return (
        dp // (sizes[X] * sizes[C]),
        dp // sizes[C] % sizes[X],
        dp % sizes[C],
        lax.axis_index("tensor"),
    )


def hop(value, sizes, digit, step=1):
    pairs = []
    nz, nx, nc, ny = sizes
    for z in range(nz):
        for x in range(nx):
            for c in range(nc):
                for y in range(ny):
                    there = [z, x, c, y]
                    there[digit] = (there[digit] + step) % sizes[digit]
                    source = ((z * nx + x) * nc + c) * ny + y
                    target = ((there[0] * nx + there[1]) * nc + there[2]) * ny + there[3]
                    pairs.append((source, target))
    return lax.ppermute(value, ALL, pairs)


def ring(value, sizes, digit):
    pieces = [value]
    for _ in range(sizes[digit] - 1):
        pieces.append(hop(pieces[-1], sizes, digit))
    return pieces


def place(pieces, index, axis):
    count = len(pieces)
    if count == 1:
        return jnp.expand_dims(pieces[0], axis)
    shape = list(pieces[0].shape)
    shape.insert(axis, count)
    out = jnp.zeros(shape, pieces[0].dtype)
    for k, piece in enumerate(pieces):
        out = lax.dynamic_update_index_in_dim(out, piece, (index - k) % count, axis)
    return out


def pick(value, index, axis):
    return lax.dynamic_index_in_dim(value, index, axis, keepdims=False)


def ring_sum(value, sizes, digit, index, axis):
    count = sizes[digit]
    if count == 1:
        return jnp.squeeze(value, axis)
    moving = pick(value, (index - 1) % count, axis)
    for k in range(1, count):
        moving = hop(moving, sizes, digit) + pick(value, (index - 1 - k) % count, axis)
    return moving


def after(value, *others):
    return lax.optimization_barrier((value, *others))[0]


def all_sum(value, sizes, digits):
    for digit in digits:
        value = sum(ring(value, sizes, digit))
    return value


def put(out, piece, x, c, begin):
    zero = jnp.int32(0)
    return lax.dynamic_update_slice(
        out, piece[:, None, None], (zero, x.astype(jnp.int32), c.astype(jnp.int32), zero, jnp.int32(begin))
    )


def gather_project(shard, sizes, at):
    half = shard.shape[1] // 2
    first = ring(shard[:, :half], sizes, X)
    second = place(ring(shard[:, half:], sizes, Z), at[Z], 0)
    first = place(ring(place(first, at[X], 0), sizes, Z), at[Z], 0)
    second = place(ring(second, sizes, X), at[X], 1)
    both = jnp.concatenate([first, second], axis=-1)
    full = place(ring(both, sizes, C), at[C], 2)
    return full.reshape(-1, shard.shape[1]), first


def spread(halves, sizes):
    if sizes[X] == 2 and sizes[Y] == 2:
        over_x = [hop(b, sizes, X) for b in halves]
        over_y = [hop(b, sizes, Y) for b in halves]
        corner = [hop(over_x[0], sizes, Y), hop(over_y[1], sizes, X)]
        return [[halves, over_x], [over_y, corner]]
    over_x = list(zip(*[ring(b, sizes, X) for b in halves]))
    both = [list(zip(*[ring(b, sizes, Y) for b in piece])) for piece in over_x]
    return [[both[j][k] for j in range(sizes[X])] for k in range(sizes[Y])]


def gather_halves(shard, sizes, at):
    deep = place(ring(shard, sizes, Z), at[Z], 0)
    half = shard.shape[1] // 2
    return spread([deep[..., :half], deep[..., half:]], sizes), deep


def assemble(pieces, sizes, at, widths):
    out = []
    for by_x in pieces:
        begins = [0]
        for width in widths:
            begins.append(begins[-1] + width)
        nz, depth, half = by_x[0][0].shape
        mats = [jnp.zeros((nz, sizes[X], sizes[C], depth, width), BF16) for width in widths]
        for j, halves in enumerate(by_x):
            for h, piece in enumerate(halves):
                for c, part in enumerate(ring(piece, sizes, C)):
                    x_at, c_at = (at[X] - j) % sizes[X], (at[C] - c) % sizes[C]
                    for m, width in enumerate(widths):
                        low = max(begins[m], h * half)
                        high = min(begins[m + 1], (h + 1) * half)
                        if low < high:
                            cut = part[..., low - h * half : high - h * half]
                            mats[m] = put(mats[m], cut, x_at, c_at, low - begins[m])
        out.append([m.reshape(-1, m.shape[-1]) for m in mats])
    return out


def core_part(fulls, sizes, core):
    return jnp.concatenate(
        [
            pick(f.reshape(sizes[Z], sizes[X], sizes[C], -1, f.shape[-1]), core, 2)
            for f in fulls
        ],
        axis=-1,
    )


def core_sum(fulls, sizes, at):
    if sizes[C] == 1:
        return core_part(fulls, sizes, at[C])
    sent = hop(core_part(fulls, sizes, (at[C] + 1) % sizes[C]), sizes, C)
    return sent + core_part(fulls, sizes, at[C])


def corner_step(parts, sizes, at):
    far_x = (at[X] + 1) % 2
    half = parts[0].shape[-1] // 2
    cut = lambda p, h: p[..., h * half : (h + 1) * half]
    own, over_x = pick(parts[0], at[X], 1), pick(parts[0], far_x, 1)
    over_y, corner = pick(parts[1], at[X], 1), pick(parts[1], far_x, 1)
    from_x = hop(cut(corner, 0), sizes, X)
    from_y = hop(cut(corner, 1), sizes, Y)
    first = hop(cut(over_x, 0), sizes, X)
    return (own, first, over_x, over_y, from_x, from_y)


def side_step(held, sizes, wait):
    own, first, over_x, over_y, from_x, from_y = held
    half = own.shape[-1] // 2
    cut = lambda p, h: p[..., h * half : (h + 1) * half]
    second = hop(cut(over_x, 1) + from_y, sizes, X)
    send = after(jnp.concatenate([cut(over_y, 0) + from_x, cut(over_y, 1)], axis=-1), *wait)
    side = hop(send, sizes, Y)
    return own + jnp.concatenate([first, second], axis=-1) + side


def plain_square(parts, sizes, at):
    total = parts[0]
    for k in range(1, sizes[Y]):
        total = total + hop(parts[k], sizes, Y, -k)
    return ring_sum(total, sizes, X, at[X], 1)


def z_steps(value, sizes, at):
    return pick(value, (at[Z] - 1) % sizes[Z], 0)


def z_next(value, moving, k, sizes, at):
    return hop(moving, sizes, Z) + pick(value, (at[Z] - 1 - k) % sizes[Z], 0)


def norm_parts(rows):
    average = jnp.mean(rows, axis=-1, keepdims=True)
    centered = rows - average
    scale = lax.rsqrt(jnp.mean(centered * centered, axis=-1, keepdims=True) + EPS)
    return centered * scale, scale


def norm_back(grad, unit, scale, gain):
    inner = grad * gain
    return scale * (
        inner
        - jnp.mean(inner, axis=-1, keepdims=True)
        - unit * jnp.mean(inner * unit, axis=-1, keepdims=True)
    )


def gelu_both(upper):
    below = 0.5 * lax.erfc(upper * -(0.5**0.5))
    density = jnp.exp(-0.5 * upper * upper) * 0.3989422804014327
    return upper * below, below + upper * density


def dot(a, b, dims):
    return lax.dot_general(a, b, (dims, ((), ())), preferred_element_type=F32)


NN = ((1,), (0,))
NT = ((1,), (1,))
TN = ((0,), (0,))


def mm(a, b):
    return jnp.dot(a, b, preferred_element_type=F32)


def turn(block):
    return block.astype(F32).T.astype(BF16)


def half_of(block, head, axis):
    return jnp.where(
        lax.broadcasted_iota(jnp.int32, block.shape, axis) // HEAD_DIM == head, block, 0
    ).astype(block.dtype)


def set_bias(down_ref, along_ref, bias_ref):
    @pl.when(pl.program_id(0) == 0)
    def _():
        bias_ref[...] = jnp.where(down_ref[...] == along_ref[...], 0.0, BIG_NEGATIVE)


def attend_kernel(q_ref, k_ref, v_ref, down_ref, along_ref, low_ref, full_ref, log_ref, bias_ref):
    set_bias(down_ref, along_ref, bias_ref)
    rows = q_ref.shape[0]
    tile = min(TILE, rows)
    turned = turn(q_ref[...].astype(F32) * HEAD_DIM ** (-0.5))
    keys = [half_of(k_ref[...], i, 1) for i in range(2)]
    values = [half_of(v_ref[...], i, 1) for i in range(2)]
    for begin in range(0, rows, tile):
        cols = slice(begin, begin + tile)
        mixed = jnp.zeros((tile, PAIR), F32)
        for i in range(2):
            scores = mm(keys[i], turned[:, cols]) + bias_ref[:, cols]
            top = jnp.max(scores, axis=0, keepdims=True)
            weights = jnp.exp(scores - top)
            total = jnp.sum(weights, axis=0, keepdims=True)
            log_ref[0, i : i + 1, cols] = top + jnp.log(total)
            mixed += dot((weights * (1.0 / total)).astype(BF16), values[i], TN)
        full_ref[cols, :] = mixed
        low_ref[cols, :] = mixed.astype(BF16)


def attend_back_kernel(
    q_ref, k_ref, v_ref, down_ref, along_ref, full_ref, log_ref, grad_ref, out_ref, bias_ref
):
    set_bias(down_ref, along_ref, bias_ref)
    rows = q_ref.shape[0]
    tile = min(TILE, rows)
    query = (q_ref[...].astype(F32) * HEAD_DIM ** (-0.5)).astype(BF16)
    grad = grad_ref[...]
    turned, grad_turned, key_turned = turn(query), turn(grad), turn(k_ref[...])
    inner = (grad.astype(F32) * full_ref[...]).T
    key_grad = jnp.zeros((rows, PAIR), F32)
    value_grad = jnp.zeros((rows, PAIR), F32)
    query_grad = [jnp.zeros((PAIR, tile), F32) for _ in range(rows // tile)]
    for i in range(2):
        key, value = half_of(k_ref[...], i, 1), half_of(v_ref[...], i, 1)
        kept_query, kept_grad = half_of(query, i, 1), half_of(grad, i, 1)
        kept_key = half_of(key_turned, i, 0)
        delta = jnp.sum(inner[i * HEAD_DIM : (i + 1) * HEAD_DIM], axis=0, keepdims=True)
        for j in range(rows // tile):
            cols = slice(j * tile, (j + 1) * tile)
            scores = mm(key, turned[:, cols]) + bias_ref[:, cols]
            probs = jnp.exp(scores - log_ref[0, i : i + 1, cols])
            prob_grad = mm(value, grad_turned[:, cols])
            score_grad = (probs * (prob_grad - delta[:, cols])).astype(BF16)
            value_grad += mm(probs.astype(BF16), kept_grad[cols])
            key_grad += mm(score_grad, kept_query[cols])
            query_grad[j] += mm(kept_key, score_grad)
    for j in range(rows // tile):
        out_ref[0, j * tile : (j + 1) * tile, :] = (query_grad[j].T * HEAD_DIM ** (-0.5)).astype(
            BF16
        )
    out_ref[1] = key_grad.astype(BF16)
    out_ref[2] = value_grad.astype(BF16)


def third(begin):
    return lambda h: (0, begin + h)


def attention(projected, segment):
    rows, width = projected.shape
    pairs = width // 3 // PAIR
    block = lambda f: pl.BlockSpec((rows, PAIR), f)
    return pl.pallas_call(
        attend_kernel,
        grid=(pairs,),
        in_specs=[block(third(c * pairs)) for c in range(3)]
        + [
            pl.BlockSpec((rows, 1), lambda h: (0, 0)),
            pl.BlockSpec((1, rows), lambda h: (0, 0)),
        ],
        out_specs=[
            block(third(0)),
            block(third(0)),
            pl.BlockSpec((1, 2, rows), lambda h: (h, 0, 0)),
        ],
        out_shape=[
            jax.ShapeDtypeStruct((rows, pairs * PAIR), BF16),
            jax.ShapeDtypeStruct((rows, pairs * PAIR), F32),
            jax.ShapeDtypeStruct((pairs, 2, rows), F32),
        ],
        scratch_shapes=[pltpu.VMEM((rows, rows), F32)],
        compiler_params=pltpu.CompilerParams(vmem_limit_bytes=40 * 2**20),
        cost_estimate=pl.CostEstimate(
            flops=pairs * 16 * rows * rows * PAIR,
            bytes_accessed=16 * rows * pairs * PAIR,
            transcendentals=2 * pairs * rows * rows,
        ),
    )(projected, projected, projected, segment[:, None], segment[None, :])


def attention_back(projected, segment, full, logs, grad, first, count):
    rows, width = projected.shape
    pairs = width // 3 // PAIR
    block = lambda f: pl.BlockSpec((rows, PAIR), f)
    return pl.pallas_call(
        attend_back_kernel,
        grid=(count,),
        in_specs=[block(third(c * pairs + first)) for c in range(3)]
        + [
            pl.BlockSpec((rows, 1), lambda h: (0, 0)),
            pl.BlockSpec((1, rows), lambda h: (0, 0)),
            block(third(first)),
            pl.BlockSpec((1, 2, rows), lambda h: (first + h, 0, 0)),
            block(third(first)),
        ],
        out_specs=pl.BlockSpec((3, rows, PAIR), lambda h: (0, 0, h)),
        out_shape=jax.ShapeDtypeStruct((3, rows, count * PAIR), BF16),
        scratch_shapes=[pltpu.VMEM((rows, rows), F32)],
        compiler_params=pltpu.CompilerParams(vmem_limit_bytes=48 * 2**20),
        cost_estimate=pl.CostEstimate(
            flops=count * 40 * rows * rows * PAIR,
            bytes_accessed=20 * rows * count * PAIR,
            transcendentals=2 * count * rows * rows,
        ),
    )(projected, projected, projected, segment[:, None], segment[None, :], full, logs, grad)


def on_device(
    tokens,
    lengths,
    project_weight,
    project_bias,
    output_weight,
    output_bias,
    first_gain,
    first_shift,
    expand_weight,
    expand_bias,
    shrink_weight,
    shrink_bias,
    second_gain,
    second_shift,
    cotangent,
):
    sizes = digit_sizes()
    at = my_digits(sizes)
    n_t = sizes[Y]
    mine = at[Y]
    rows, width = tokens.shape
    all_rows = rows * n_t
    heads_width = project_weight.shape[2]
    hidden = expand_weight.shape[1]
    depth = project_weight.shape[1]
    pairs = heads_width // PAIR
    square = sizes[X] == 2 and n_t == 2

    ends = jnp.cumsum(lengths[0], dtype=jnp.int32)
    positions = lax.iota(jnp.int32, all_rows)
    segment = jnp.sum(
        (positions[:, None] >= ends[None, :]).astype(jnp.int32), axis=1, dtype=jnp.int32
    )
    valid = (mine * rows + lax.iota(jnp.int32, rows) < ends[-1])[:, None]

    whole_tokens = place(ring(tokens, sizes, Y), mine, 0).reshape(all_rows, width)
    proj, early = gather_project(
        jnp.transpose(project_weight, (1, 0, 2)).reshape(depth, 3 * heads_width), sizes, at
    )
    upper_shard = jnp.concatenate([output_weight.T, expand_weight], axis=1)
    upper_pieces, deep = gather_halves(after(upper_shard, early), sizes, at)
    shrink_pieces, _ = gather_halves(after(shrink_weight.T, deep), sizes, at)
    expand_biases = ring(expand_bias, sizes, Y)

    bias = jnp.concatenate([project_bias[0], jnp.zeros_like(project_bias[0]), project_bias[1]])
    projected = (dot(whole_tokens, proj, NN) + bias).astype(BF16)
    mixed_low, mixed_full, logs = attention(projected, segment)
    by_rows = mixed_low.reshape(n_t, rows, heads_width)
    mixed = [pick(by_rows, mine, 0)]
    for k in range(1, n_t):
        mixed.append(hop(pick(by_rows, (mine + k) % n_t, 0), sizes, Y, k))

    gathered = assemble(upper_pieces, sizes, at, (heads_width, hidden))
    mix = [g[0] for g in gathered]
    expand = [g[1] for g in gathered]
    attn = sum(dot(m, w, NT) for m, w in zip(mixed, mix)) + output_bias
    unit1, scale1 = norm_parts(tokens.astype(F32) + attn)
    normed1 = unit1 * first_gain + first_shift
    low1 = normed1.astype(BF16)
    active, slope = [], []
    for w, b in zip(expand, expand_biases):
        act, der = gelu_both(dot(low1, w, NN) + b)
        active.append(act.astype(BF16))
        slope.append(der.astype(BF16))
    shrink = [g[0] for g in assemble(shrink_pieces, sizes, at, (hidden,))]
    branch = sum(dot(a, w, NT) for a, w in zip(active, shrink)) + shrink_bias
    unit2, scale2 = norm_parts(normed1 + branch)
    layer_output = jnp.where(valid, unit2 * second_gain + second_shift, 0.0).astype(BF16)

    grad = jnp.where(valid, cotangent.astype(F32), 0.0)
    grad_second_gain = jnp.sum(grad * unit2, axis=0)
    grad_second_shift = jnp.sum(grad, axis=0)
    grad_r2 = norm_back(grad, unit2, scale2, second_gain)
    grad_branch = grad_r2.astype(BF16)
    grad_shrink_bias = jnp.sum(grad_branch, axis=0, dtype=F32)
    shrink_parts = [core_sum([dot(grad_branch, a, TN).astype(BF16)], sizes, at) for a in active]
    grad_upper = [
        (dot(grad_branch, w, NN) * s.astype(F32)).astype(BF16) for w, s in zip(shrink, slope)
    ]
    grad_expand_biases = [jnp.sum(g, axis=0, dtype=F32) for g in grad_upper]
    if square:
        shrink_held = corner_step(shrink_parts, sizes, at)
    low1_later = after(low1, *shrink_parts)
    grad_expand = [dot(low1_later, g, TN).astype(BF16) for g in grad_upper]
    expand_parts = [core_sum([g], sizes, at) for g in grad_expand]
    grad_normed1 = sum(dot(g, w, NT) for g, w in zip(grad_upper, expand)) + grad_r2
    if square:
        grad_normed1 = after(grad_normed1, *shrink_held)
    grad_first_gain = jnp.sum(grad_normed1 * unit1, axis=0)
    grad_first_shift = jnp.sum(grad_normed1, axis=0)
    grad_r1 = norm_back(grad_normed1, unit1, scale1, first_gain)
    grad_attn = grad_r1.astype(BF16)
    grad_output_bias = jnp.sum(grad_attn, axis=0, dtype=F32)

    grad_pieces = []
    for k, w in enumerate(mix):
        part = dot(grad_attn, w, NN).astype(BF16)
        grad_pieces.append(hop(part, sizes, Y, -k) if k else part)
    grad_rows = place([grad_pieces[-k % n_t] for k in range(n_t)], mine, 0)
    grad_rows = grad_rows.reshape(all_rows, heads_width)
    grad_mix = [dot(grad_attn, m, TN).astype(BF16) for m in mixed]
    upper_parts = [
        jnp.concatenate([core_sum([a], sizes, at), b], axis=-1)
        for a, b in zip(grad_mix, expand_parts)
    ]
    calls = 2 if pairs % 2 == 0 else 1
    if square:
        upper_held = corner_step(upper_parts, sizes, at)
        shrink_sum = side_step(shrink_held, sizes, (grad_rows,))
        grad_rows = after(grad_rows, *upper_parts)
    else:
        shrink_sum = plain_square(shrink_parts, sizes, at)
        upper_sum = plain_square(upper_parts, sizes, at)
    done = [
        attention_back(
            projected, segment, mixed_full, logs, grad_rows, 0, pairs // calls
        )
    ]
    if square:
        upper_sum = side_step(upper_held, sizes, (done[0],))
        logs = after(logs, done[0], *upper_held)
    if calls == 2:
        done.append(
            attention_back(
                projected, segment, mixed_full, logs, grad_rows, pairs // 2, pairs // 2
            )
        )
    projected_grad = jnp.concatenate(done, axis=-1)
    moving = z_steps(shrink_sum, sizes, at)
    if sizes[Z] > 1:
        moving = z_next(shrink_sum, moving, 1, sizes, at)
        projected_grad = after(projected_grad, shrink_sum)

    project_parts = [
        dot(whole_tokens, projected_grad[c], TN).astype(BF16) for c in range(3)
    ]
    bias_sums = jnp.stack(
        [jnp.sum(projected_grad[c], axis=0, dtype=F32) for c in (0, 2)]
    )
    project_sum = core_sum(project_parts, sizes, at)
    cut = 3 * heads_width // 2
    first_half = ring_sum(project_sum[..., :cut], sizes, X, at[X], 1)
    second_half = ring_sum(project_sum[..., cut:], sizes, Z, at[Z], 0)
    first_half = ring_sum(first_half, sizes, Z, at[Z], 0)
    second_half = ring_sum(second_half, sizes, X, at[X], 0)
    grad_project = jnp.concatenate([first_half, second_half], axis=-1)
    grad_project_weight = jnp.transpose(
        grad_project.reshape(depth, 3, heads_width), (1, 0, 2)
    ).astype(F32)
    grad_project_bias = all_sum(bias_sums, sizes, (C, X, Z))

    for k in range(2, sizes[Z]):
        moving = z_next(shrink_sum, moving, k, sizes, at)
    grad_shrink_weight = moving.astype(F32).T
    owned = ring_sum(upper_sum, sizes, Z, at[Z], 0).astype(F32)
    grad_output_weight = owned[:, :heads_width].T
    grad_expand_weight = owned[:, heads_width:]

    packed = jnp.concatenate(
        [
            grad_second_gain,
            grad_second_shift,
            grad_shrink_bias,
            grad_first_gain,
            grad_first_shift,
            grad_output_bias,
            place(grad_expand_biases, mine, 0).reshape(-1),
        ]
    )
    packed = all_sum(packed, sizes, (C, X, Y, Z))
    (
        grad_second_gain,
        grad_second_shift,
        grad_shrink_bias,
        grad_first_gain,
        grad_first_shift,
        grad_output_bias,
    ) = (packed[i * width : (i + 1) * width] for i in range(6))
    grad_expand_bias = pick(packed[6 * width :].reshape(n_t, hidden), mine, 0)

    proj_cube = proj.reshape(width, 3, heads_width)
    token_grad = grad_r1
    for k in range(n_t):
        begin = (mine + k) % n_t * rows
        part = lax.dot_general(
            lax.dynamic_slice_in_dim(projected_grad, begin, rows, 1),
            proj_cube,
            (((0, 2), (1, 2)), ((), ())),
            preferred_element_type=F32,
        )
        if k:
            part = hop(part.astype(BF16), sizes, Y, k).astype(F32)
        token_grad = token_grad + part
    grad_tokens = token_grad.astype(BF16)
    return (
        layer_output,
        grad_tokens,
        grad_project_weight,
        grad_project_bias,
        grad_output_weight,
        grad_output_bias,
        grad_first_gain,
        grad_first_shift,
        grad_expand_weight,
        grad_expand_bias,
        grad_shrink_weight,
        grad_shrink_bias,
        grad_second_gain,
        grad_second_shift,
    )


def solution(mesh):
    rows = P(("dp", "tensor"), None)
    weights = (P(None, "dp", "tensor"), P("tensor", "dp"), P("dp", "tensor"), P("tensor", "dp"))
    in_specs = (
        rows,
        P("dp", None),
        weights[0],
        P(None, "tensor"),
        weights[1],
        P(),
        P(),
        P(),
        weights[2],
        P("tensor"),
        weights[3],
        P(),
        P(),
        P(),
        rows,
    )
    out_specs = (
        rows,
        rows,
        weights[0],
        P(None, "tensor"),
        weights[1],
        P(),
        P(),
        P(),
        weights[2],
        P("tensor"),
        weights[3],
        P(),
        P(),
        P(),
    )
    return jax.shard_map(
        on_device, mesh=mesh, in_specs=in_specs, out_specs=out_specs, check_vma=False
    )
```

```python
import jax
import jax.numpy as jnp
from jax import lax
from jax.experimental import pallas as pl
from jax.experimental.pallas import tpu as pltpu
from jax.sharding import PartitionSpec as P

HEAD_DIM = 64
TILE = 256
PAIR = 2 * HEAD_DIM
EPS = 1e-05
BIG_NEGATIVE = -1e30
ALL = ("dp", "tensor")
Z, X, C, Y = range(4)
F32 = jnp.float32
BF16 = jnp.bfloat16


def digit_sizes():
    rest = lax.axis_size("dp")
    core = 2 if rest % 2 == 0 else 1
    rest //= core
    across = 2 if rest % 2 == 0 else 1
    rest //= across
    return (rest, across, core, lax.axis_size("tensor"))


def my_digits(sizes):
    dp = lax.axis_index("dp")
    return (
        dp // (sizes[X] * sizes[C]),
        dp // sizes[C] % sizes[X],
        dp % sizes[C],
        lax.axis_index("tensor"),
    )


def hop(value, sizes, digit, step=1):
    pairs = []
    nz, nx, nc, ny = sizes
    for z in range(nz):
        for x in range(nx):
            for c in range(nc):
                for y in range(ny):
                    there = [z, x, c, y]
                    there[digit] = (there[digit] + step) % sizes[digit]
                    source = ((z * nx + x) * nc + c) * ny + y
                    target = ((there[0] * nx + there[1]) * nc + there[2]) * ny + there[3]
                    pairs.append((source, target))
    return lax.ppermute(value, ALL, pairs)


def ring(value, sizes, digit):
    pieces = [value]
    for _ in range(sizes[digit] - 1):
        pieces.append(hop(pieces[-1], sizes, digit))
    return pieces


def place(pieces, index, axis):
    count = len(pieces)
    if count == 1:
        return jnp.expand_dims(pieces[0], axis)
    shape = list(pieces[0].shape)
    shape.insert(axis, count)
    out = jnp.zeros(shape, pieces[0].dtype)
    for k, piece in enumerate(pieces):
        out = lax.dynamic_update_index_in_dim(out, piece, (index - k) % count, axis)
    return out


def pick(value, index, axis):
    return lax.dynamic_index_in_dim(value, index, axis, keepdims=False)


def spread_sum(value, sizes, digit, index, axis):
    count = sizes[digit]
    terms = [pick(value, index, axis)]
    for k in range(1, count):
        terms.append(hop(pick(value, (index + k) % count, axis), sizes, digit, k))
    return terms


def sum_over(value, sizes, digit, index, axis):
    return sum(spread_sum(value, sizes, digit, index, axis))


def sync(*values):
    return lax.optimization_barrier(values)


def all_sum(value, sizes, digit):
    return value + sum(hop(value, sizes, digit, k) for k in range(1, sizes[digit]))


def fan(value, sizes, digit):
    return [value] + [hop(value, sizes, digit, k) for k in range(1, sizes[digit])]


def arrange(pieces, shapes, moves, places):
    out = [jnp.zeros(shape, BF16) for shape in shapes]
    for source, low, width, target, begin, lead in moves:
        piece = pieces[source][..., low : low + width]
        start = [jnp.int32(0) if w is None else places[w].astype(jnp.int32) for w in lead]
        fixed = [n for n, w in enumerate(lead) if w is not None]
        piece = jnp.expand_dims(piece, fixed)
        start += [jnp.int32(0), jnp.int32(begin)]
        out[target] = lax.dynamic_update_slice(out[target], piece, start)
    return out


def gather_project(shard, sizes, at, later):
    half = shard.shape[1] // 2
    over_x = hop(shard[:, :half], sizes, X) if sizes[X] == 2 else None
    second = place(fan(shard[:, half:], sizes, Z), at[Z], 0)
    first = [shard[:, :half]] + ([over_x] if sizes[X] == 2 else [])
    first = fan(place(first, at[X], 0), sizes, Z)
    first, later = sync(first, later)
    first = place(first, at[Z], 0)
    second = place(fan(second, sizes, X), at[X], 1)
    both = jnp.concatenate([first, second], axis=-1)
    full = place(fan(both, sizes, C), at[C], 2)
    return full.reshape(-1, shard.shape[1]), later


def stack_z(pieces, sizes, at):
    depth, width = pieces[0].shape
    cut = (width // 2 + 127) // 128 * 128
    shapes = [(sizes[Z], depth, cut), (sizes[Z], depth, width - cut)]
    moves = []
    for k in range(sizes[Z]):
        moves.append((k, 0, cut, 0, 0, (k,)))
        moves.append((k, cut, width - cut, 1, 0, (k,)))
    return arrange(pieces, shapes, moves, [(at[Z] - k) % sizes[Z] for k in range(sizes[Z])])


def spread_sides(halves, sizes):
    over_x = list(zip(*[fan(b, sizes, X) for b in halves]))
    if sizes[X] == 2 and sizes[Y] == 2:
        return over_x, [hop(b, sizes, Y) for b in halves]
    return over_x, []


def spread_corner(over_x, over_y, sizes):
    if sizes[X] == 2 and sizes[Y] == 2:
        corner = [hop(over_x[1][0], sizes, Y), hop(over_y[1], sizes, X)]
        return [list(over_x), [over_y, corner]]
    both = [list(zip(*[fan(b, sizes, Y) for b in piece])) for piece in over_x]
    return [[both[j][k] for j in range(sizes[X])] for k in range(sizes[Y])]


def assemble(spreads, sizes, at, widths):
    begins = [sum(widths[:m]) for m in range(len(widths))]
    nz, depth, _ = spreads[0][0][0].shape
    pieces, moves, shapes = [], [], []
    for k, by_x in enumerate(spreads):
        shapes += [(nz, sizes[X], sizes[C], depth, width) for width in widths]
        for j, halves in enumerate(by_x):
            base = 0
            for half in halves:
                size = half.shape[-1]
                for c, part in enumerate(fan(half, sizes, C)):
                    for m, width in enumerate(widths):
                        low = max(begins[m], base)
                        high = min(begins[m] + width, base + size)
                        if low < high:
                            lead = (None, j, sizes[X] + c)
                            target = k * len(widths) + m
                            moves.append(
                                (len(pieces), low - base, high - low, target, low - begins[m], lead)
                            )
                    pieces.append(part)
                base += size
    places = [(at[X] - j) % sizes[X] for j in range(sizes[X])]
    places += [(at[C] - c) % sizes[C] for c in range(sizes[C])]
    mats = arrange(pieces, shapes, moves, places)
    mats = [m.reshape(-1, m.shape[-1]) for m in mats]
    count = len(widths)
    return [mats[k * count : (k + 1) * count] for k in range(len(spreads))]


def core_part(full, sizes, core):
    return pick(full.reshape(sizes[Z], sizes[X], sizes[C], -1, full.shape[-1]), core, 2)


def core_send(full, sizes, at):
    own = core_part(full, sizes, at[C])
    if sizes[C] == 1:
        return (own,)
    return (hop(core_part(full, sizes, (at[C] + 1) % sizes[C]), sizes, C), own)


def corner_step(parts, sizes, at):
    far_x = (at[X] + 1) % 2
    half = parts[0].shape[-1] // 2
    cut = lambda p, h: p[..., h * half : (h + 1) * half]
    own, over_x = pick(parts[0], at[X], 1), pick(parts[0], far_x, 1)
    over_y, corner = pick(parts[1], at[X], 1), pick(parts[1], far_x, 1)
    from_x = hop(cut(corner, 0), sizes, X)
    from_y = hop(cut(corner, 1), sizes, Y)
    return (own, over_x, over_y, from_x, from_y)


def side_step(held, sizes):
    own, over_x, over_y, from_x, from_y = held
    half = own.shape[-1] // 2
    cut = lambda p, h: p[..., h * half : (h + 1) * half]
    to_x = jnp.concatenate([cut(over_x, 0), cut(over_x, 1) + from_y], axis=-1)
    to_y = jnp.concatenate([cut(over_y, 0) + from_x, cut(over_y, 1)], axis=-1)
    return (own, hop(to_x, sizes, X), hop(to_y, sizes, Y))


def plain_square(parts, sizes, at):
    total = parts[0]
    for k in range(1, sizes[Y]):
        total = total + hop(parts[k], sizes, Y, -k)
    return (sum_over(total, sizes, X, at[X], 1),)


def norm_parts(rows):
    average = jnp.mean(rows, axis=-1, keepdims=True)
    centered = rows - average
    scale = lax.rsqrt(jnp.mean(centered * centered, axis=-1, keepdims=True) + EPS)
    return centered * scale, scale


def norm_back(grad, unit, scale, gain):
    inner = grad * gain
    return scale * (
        inner
        - jnp.mean(inner, axis=-1, keepdims=True)
        - unit * jnp.mean(inner * unit, axis=-1, keepdims=True)
    )


def gelu_both(upper):
    below = 0.5 * lax.erfc(upper * -(0.5**0.5))
    density = jnp.exp(-0.5 * upper * upper) * 0.3989422804014327
    return upper * below, below + upper * density


def dot(a, b, dims):
    return lax.dot_general(a, b, (dims, ((), ())), preferred_element_type=F32)


NN = ((1,), (0,))
NT = ((1,), (1,))
TN = ((0,), (0,))


def mm(a, b):
    return jnp.dot(a, b, preferred_element_type=F32)


def turn(block):
    return block.astype(F32).T.astype(BF16)


def half_of(block, head, axis):
    return jnp.where(
        lax.broadcasted_iota(jnp.int32, block.shape, axis) // HEAD_DIM == head, block, 0
    ).astype(block.dtype)


def set_bias(down_ref, along_ref, bias_ref):
    @pl.when(pl.program_id(0) == 0)
    def _():
        bias_ref[...] = jnp.where(down_ref[...] == along_ref[...], 0.0, BIG_NEGATIVE)


def attend_kernel(q_ref, k_ref, v_ref, down_ref, along_ref, low_ref, full_ref, log_ref, bias_ref):
    set_bias(down_ref, along_ref, bias_ref)
    rows = q_ref.shape[0]
    tile = min(TILE, rows)
    turned = turn(q_ref[...].astype(F32) * HEAD_DIM ** (-0.5))
    keys = [half_of(k_ref[...], i, 1) for i in range(2)]
    values = [half_of(v_ref[...], i, 1) for i in range(2)]
    for begin in range(0, rows, tile):
        cols = slice(begin, begin + tile)
        mixed = jnp.zeros((tile, PAIR), F32)
        for i in range(2):
            scores = mm(keys[i], turned[:, cols]) + bias_ref[:, cols]
            top = jnp.max(scores, axis=0, keepdims=True)
            weights = jnp.exp(scores - top)
            total = jnp.sum(weights, axis=0, keepdims=True)
            log_ref[0, i : i + 1, cols] = top + jnp.log(total)
            mixed += dot((weights * (1.0 / total)).astype(BF16), values[i], TN)
        full_ref[cols, :] = mixed
        low_ref[cols, :] = mixed.astype(BF16)


def attend_back_kernel(
    q_ref, k_ref, v_ref, down_ref, along_ref, full_ref, log_ref, grad_ref, out_ref, bias_ref
):
    set_bias(down_ref, along_ref, bias_ref)
    rows = q_ref.shape[0]
    tile = min(TILE, rows)
    query = (q_ref[...].astype(F32) * HEAD_DIM ** (-0.5)).astype(BF16)
    grad = grad_ref[...]
    turned, grad_turned, key_turned = turn(query), turn(grad), turn(k_ref[...])
    inner = (grad.astype(F32) * full_ref[...]).T
    key_grad = jnp.zeros((rows, PAIR), F32)
    value_grad = jnp.zeros((rows, PAIR), F32)
    query_grad = [jnp.zeros((PAIR, tile), F32) for _ in range(rows // tile)]
    for i in range(2):
        key, value = half_of(k_ref[...], i, 1), half_of(v_ref[...], i, 1)
        kept_query, kept_grad = half_of(query, i, 1), half_of(grad, i, 1)
        kept_key = half_of(key_turned, i, 0)
        delta = jnp.sum(inner[i * HEAD_DIM : (i + 1) * HEAD_DIM], axis=0, keepdims=True)
        for j in range(rows // tile):
            cols = slice(j * tile, (j + 1) * tile)
            scores = mm(key, turned[:, cols]) + bias_ref[:, cols]
            probs = jnp.exp(scores - log_ref[0, i : i + 1, cols])
            prob_grad = mm(value, grad_turned[:, cols])
            score_grad = (probs * (prob_grad - delta[:, cols])).astype(BF16)
            value_grad += mm(probs.astype(BF16), kept_grad[cols])
            key_grad += mm(score_grad, kept_query[cols])
            query_grad[j] += mm(kept_key, score_grad)
    for j in range(rows // tile):
        out_ref[0, j * tile : (j + 1) * tile, :] = (query_grad[j].T * HEAD_DIM ** (-0.5)).astype(
            BF16
        )
    out_ref[1] = key_grad.astype(BF16)
    out_ref[2] = value_grad.astype(BF16)


def third(begin):
    return lambda h: (0, begin + h)


def attention(projected, segment, first, count):
    rows, width = projected.shape
    pairs = width // 3 // PAIR
    block = lambda f: pl.BlockSpec((rows, PAIR), f)
    return pl.pallas_call(
        attend_kernel,
        grid=(count,),
        in_specs=[block(third(c * pairs + first)) for c in range(3)]
        + [
            pl.BlockSpec((rows, 1), lambda h: (0, 0)),
            pl.BlockSpec((1, rows), lambda h: (0, 0)),
        ],
        out_specs=[
            block(third(0)),
            block(third(0)),
            pl.BlockSpec((1, 2, rows), lambda h: (h, 0, 0)),
        ],
        out_shape=[
            jax.ShapeDtypeStruct((rows, count * PAIR), BF16),
            jax.ShapeDtypeStruct((rows, count * PAIR), F32),
            jax.ShapeDtypeStruct((count, 2, rows), F32),
        ],
        scratch_shapes=[pltpu.VMEM((rows, rows), F32)],
        compiler_params=pltpu.CompilerParams(vmem_limit_bytes=40 * 2**20),
        cost_estimate=pl.CostEstimate(
            flops=count * 16 * rows * rows * PAIR,
            bytes_accessed=16 * rows * count * PAIR,
            transcendentals=2 * count * rows * rows,
        ),
    )(projected, projected, projected, segment[:, None], segment[None, :])


def attention_back(projected, segment, full, logs, grad, first, count):
    rows, width = projected.shape
    pairs = width // 3 // PAIR
    block = lambda f: pl.BlockSpec((rows, PAIR), f)
    return pl.pallas_call(
        attend_back_kernel,
        grid=(count,),
        in_specs=[block(third(c * pairs + first)) for c in range(3)]
        + [
            pl.BlockSpec((rows, 1), lambda h: (0, 0)),
            pl.BlockSpec((1, rows), lambda h: (0, 0)),
            block(third(0)),
            pl.BlockSpec((1, 2, rows), lambda h: (h, 0, 0)),
            block(third(first)),
        ],
        out_specs=pl.BlockSpec((3, rows, PAIR), lambda h: (0, 0, h)),
        out_shape=jax.ShapeDtypeStruct((3, rows, count * PAIR), BF16),
        scratch_shapes=[pltpu.VMEM((rows, rows), F32)],
        compiler_params=pltpu.CompilerParams(vmem_limit_bytes=48 * 2**20),
        cost_estimate=pl.CostEstimate(
            flops=count * 40 * rows * rows * PAIR,
            bytes_accessed=20 * rows * count * PAIR,
            transcendentals=2 * count * rows * rows,
        ),
    )(projected, projected, projected, segment[:, None], segment[None, :], full, logs, grad)


def on_device(
    tokens,
    lengths,
    project_weight,
    project_bias,
    output_weight,
    output_bias,
    first_gain,
    first_shift,
    expand_weight,
    expand_bias,
    shrink_weight,
    shrink_bias,
    second_gain,
    second_shift,
    cotangent,
):
    sizes = digit_sizes()
    at = my_digits(sizes)
    n_t = sizes[Y]
    mine = at[Y]
    rows, width = tokens.shape
    all_rows = rows * n_t
    heads_width = project_weight.shape[2]
    hidden = expand_weight.shape[1]
    depth = project_weight.shape[1]
    pairs = heads_width // PAIR
    square = sizes[X] == 2 and n_t == 2

    ends = jnp.cumsum(lengths[0], dtype=jnp.int32)
    positions = lax.iota(jnp.int32, all_rows)
    segment = jnp.sum(
        (positions[:, None] >= ends[None, :]).astype(jnp.int32), axis=1, dtype=jnp.int32
    )
    valid = (mine * rows + lax.iota(jnp.int32, rows) < ends[-1])[:, None]

    calls = 2 if pairs % 2 == 0 else 1
    group = pairs // calls
    span = group * PAIR

    token_pieces = fan(tokens, sizes, Y)
    upper_shard = jnp.concatenate([output_weight.T, expand_weight], axis=1)
    proj, (upper_shard, token_pieces) = gather_project(
        jnp.transpose(project_weight, (1, 0, 2)).reshape(depth, 3 * heads_width),
        sizes,
        at,
        (upper_shard, token_pieces),
    )
    whole_tokens = place(token_pieces, mine, 0).reshape(all_rows, width)
    upper_z = fan(upper_shard, sizes, Z)
    expand_biases = fan(expand_bias, sizes, Y)

    bias = jnp.concatenate([project_bias[0], jnp.zeros_like(project_bias[0]), project_bias[1]])
    projected = (dot(whole_tokens, proj, NN) + bias).astype(BF16)
    projected, shrink_shard = sync(projected, shrink_weight.T)
    shrink_z = fan(shrink_shard, sizes, Z)
    fwd = [attention(projected, segment, 0, group)]
    fwd[0], upper_z, projected = sync(fwd[0], upper_z, projected)
    upper_x, upper_y = spread_sides(stack_z(upper_z, sizes, at), sizes)
    if calls == 2:
        fwd.append(attention(projected, segment, group, group))
    if square:
        fwd[-1], upper_x[1], upper_y = sync(fwd[-1], upper_x[1], upper_y)
    by_rows = jnp.concatenate([f[0] for f in fwd], axis=1).reshape(n_t, rows, heads_width)
    mixed = [pick(by_rows, mine, 0)]
    for k in range(1, n_t):
        mixed.append(hop(pick(by_rows, (mine + k) % n_t, 0), sizes, Y, k))

    upper_pieces = spread_corner(upper_x, upper_y, sizes)
    mixed, shrink_z = sync(mixed, shrink_z)
    shrink_x, shrink_y = spread_sides(stack_z(shrink_z, sizes, at), sizes)
    gathered = assemble(upper_pieces, sizes, at, (heads_width, hidden))
    mix = [g[0] for g in gathered]
    expand = [g[1] for g in gathered]
    attn = sum(dot(m, w, NT) for m, w in zip(mixed, mix)) + output_bias
    unit1, scale1 = norm_parts(tokens.astype(F32) + attn)
    normed1 = unit1 * first_gain + first_shift
    low1 = normed1.astype(BF16)
    active, slope = [], []
    low1_now = low1
    for w, b in zip(expand, expand_biases):
        act, der = gelu_both(dot(low1_now, w, NN) + b)
        active.append(act.astype(BF16))
        slope.append(der.astype(BF16))
        if len(active) == 1:
            active[0], low1_now, shrink_x, shrink_y = sync(active[0], low1, shrink_x, shrink_y)
    shrink_pieces = spread_corner(shrink_x, shrink_y, sizes)
    shrink = [g[0] for g in assemble(shrink_pieces, sizes, at, (hidden,))]
    branch = sum(dot(a, w, NT) for a, w in zip(active, shrink)) + shrink_bias
    unit2, scale2 = norm_parts(normed1 + branch)
    layer_output = jnp.where(valid, unit2 * second_gain + second_shift, 0.0).astype(BF16)

    grad = jnp.where(valid, cotangent.astype(F32), 0.0)
    grad_second_gain = jnp.sum(grad * unit2, axis=0)
    grad_second_shift = jnp.sum(grad, axis=0)
    grad_r2 = norm_back(grad, unit2, scale2, second_gain)
    grad_branch = grad_r2.astype(BF16)
    grad_shrink_bias = jnp.sum(grad_branch, axis=0, dtype=F32)
    shrink_core = [core_send(dot(grad_branch, a, TN).astype(BF16), sizes, at) for a in active]
    grad_upper = [
        (dot(grad_branch, w, NN) * s.astype(F32)).astype(BF16) for w, s in zip(shrink, slope)
    ]
    grad_expand_biases = [jnp.sum(g, axis=0, dtype=F32) for g in grad_upper]
    grad_normed1 = sum(dot(g, w, NT) for g, w in zip(grad_upper, expand)) + grad_r2
    shrink_core, grad_normed1 = sync(shrink_core, grad_normed1)
    shrink_parts = [sum(parts) for parts in shrink_core]
    if square:
        shrink_held = corner_step(shrink_parts, sizes, at)
    grad_first_gain = jnp.sum(grad_normed1 * unit1, axis=0)
    grad_first_shift = jnp.sum(grad_normed1, axis=0)
    grad_r1 = norm_back(grad_normed1, unit1, scale1, first_gain)
    grad_attn = grad_r1.astype(BF16)
    grad_output_bias = jnp.sum(grad_attn, axis=0, dtype=F32)

    grad_pieces = []
    for k, w in enumerate(mix):
        part = dot(grad_attn, w, NN).astype(BF16)
        grad_pieces.append(hop(part, sizes, Y, -k) if k else part)
    low1, grad_attn = sync(low1, grad_attn)
    grad_expand = [dot(low1, g, TN).astype(BF16) for g in grad_upper]
    if square:
        grad_expand, shrink_held = sync(grad_expand, shrink_held)
        shrink_sides = side_step(shrink_held, sizes)
    else:
        shrink_sides = plain_square(shrink_parts, sizes, at)
    expand_core = [core_send(g, sizes, at) for g in grad_expand]
    grad_mix = [dot(grad_attn, m, TN).astype(BF16) for m in mixed]
    mix_core = [core_send(g, sizes, at) for g in grad_mix]
    grad_rows = place([grad_pieces[-k % n_t] for k in range(n_t)], mine, 0)
    grad_rows = grad_rows.reshape(all_rows, heads_width)
    packed = jnp.concatenate(
        [
            grad_second_gain,
            grad_second_shift,
            grad_shrink_bias,
            grad_first_gain,
            grad_first_shift,
            grad_output_bias,
            place(grad_expand_biases, mine, 0).reshape(-1),
        ]
    )
    grad_rows, mix_core, expand_core, packed = sync(grad_rows, mix_core, expand_core, packed)
    upper_parts = [
        jnp.concatenate([sum(a), sum(b)], axis=-1) for a, b in zip(mix_core, expand_core)
    ]
    if square:
        upper_held = corner_step(upper_parts, sizes, at)
    else:
        upper_sides = plain_square(upper_parts, sizes, at)
    packed = all_sum(packed, sizes, C)

    back = []
    project_sums = []
    bias_sums = []
    for n in range(calls):
        low, full, logs = fwd[n]
        part = attention_back(projected, segment, full, logs, grad_rows, n * group, group)
        if n == 0:
            if square:
                part, shrink_sides, upper_held, packed, grad_rows = sync(
                    part, shrink_sides, upper_held, packed, grad_rows
                )
                upper_sides = side_step(upper_held, sizes)
            shrink_z = spread_sum(sum(shrink_sides), sizes, Z, at[Z], 0)
            packed = all_sum(packed, sizes, X)
        back.append(part)
        columns = jnp.concatenate([part[c] for c in range(3)], axis=-1)
        bias_sums.append(jnp.sum(columns, axis=0, dtype=F32))
        project_sums.append(core_send(dot(whole_tokens, columns, TN).astype(BF16), sizes, at))
        if n == 0:
            project_sums[0], grad_rows = sync(project_sums[0], grad_rows)
            project_x = [spread_sum(sum(project_sums[0]), sizes, X, at[X], 1)]
    projected_grad = jnp.concatenate([b[c] for c in range(3) for b in back], axis=-1)
    bias_sum = jnp.concatenate([b.reshape(3, span) for b in bias_sums], axis=-1)
    bias_sum = jnp.stack([bias_sum[0], bias_sum[2]]).reshape(-1)
    bias_sum = all_sum(bias_sum, sizes, C)
    token_parts = []
    for k in range(n_t):
        begin = (mine + k) % n_t * rows
        part = dot(lax.dynamic_slice_in_dim(projected_grad, begin, rows, 0), proj, NT)
        token_parts.append(part.astype(BF16) if k else part)
    project_sums, project_x, upper_sides, shrink_z, token_parts, packed, bias_sum = sync(
        project_sums, project_x, upper_sides, shrink_z, token_parts, packed, bias_sum
    )
    token_parts = [hop(p, sizes, Y, k).astype(F32) if k else p for k, p in enumerate(token_parts)]
    packed = all_sum(packed, sizes, Y)
    bias_sum = all_sum(bias_sum, sizes, X)
    grad_shrink_weight = sum(shrink_z).astype(F32).T
    owned_upper = spread_sum(sum(upper_sides), sizes, Z, at[Z], 0)
    owned = [spread_sum(sum(project_x[0]), sizes, Z, at[Z], 0)]
    for parts in project_sums[1:]:
        total = sum_over(sum(parts), sizes, X, at[X], 1)
        total, owned_upper, owned[0], packed, bias_sum = sync(
            total, owned_upper, owned[0], packed, bias_sum
        )
        owned.append(spread_sum(total, sizes, Z, at[Z], 0))
    owned = [sum(o).reshape(depth, 3, span) for o in owned]
    grad_project_weight = jnp.transpose(
        jnp.concatenate(owned, axis=-1), (1, 0, 2)
    ).astype(F32)
    owned = sum(owned_upper).astype(F32)
    grad_output_weight = owned[:, :heads_width].T
    grad_expand_weight = owned[:, heads_width:]

    packed = all_sum(jnp.concatenate([packed, bias_sum]), sizes, Z)
    grad_project_bias = packed[-bias_sum.shape[0] :].reshape(2, heads_width)
    packed = packed[: -bias_sum.shape[0]]
    (
        grad_second_gain,
        grad_second_shift,
        grad_shrink_bias,
        grad_first_gain,
        grad_first_shift,
        grad_output_bias,
    ) = (packed[i * width : (i + 1) * width] for i in range(6))
    grad_expand_bias = pick(packed[6 * width :].reshape(n_t, hidden), mine, 0)
    grad_tokens = (grad_r1 + sum(token_parts)).astype(BF16)
    return (
        layer_output,
        grad_tokens,
        grad_project_weight,
        grad_project_bias,
        grad_output_weight,
        grad_output_bias,
        grad_first_gain,
        grad_first_shift,
        grad_expand_weight,
        grad_expand_bias,
        grad_shrink_weight,
        grad_shrink_bias,
        grad_second_gain,
        grad_second_shift,
    )


def solution(mesh):
    rows = P(("dp", "tensor"), None)
    weights = (P(None, "dp", "tensor"), P("tensor", "dp"), P("dp", "tensor"), P("tensor", "dp"))
    in_specs = (
        rows,
        P("dp", None),
        weights[0],
        P(None, "tensor"),
        weights[1],
        P(),
        P(),
        P(),
        weights[2],
        P("tensor"),
        weights[3],
        P(),
        P(),
        P(),
        rows,
    )
    out_specs = (
        rows,
        rows,
        weights[0],
        P(None, "tensor"),
        weights[1],
        P(),
        P(),
        P(),
        weights[2],
        P("tensor"),
        weights[3],
        P(),
        P(),
        P(),
    )
    return jax.shard_map(
        on_device, mesh=mesh, in_specs=in_specs, out_specs=out_specs, check_vma=False
    )
```

```python
import jax
import jax.numpy as jnp
from jax import lax
from jax.experimental import pallas as pl
from jax.experimental.pallas import tpu as pltpu
from jax.sharding import PartitionSpec as P

HEAD_DIM = 64
TILE = 256
PAIR = 2 * HEAD_DIM
EPS = 1e-05
BIG_NEGATIVE = -1e30
ALL = ("dp", "tensor")
Z, X, C, Y = range(4)
F32 = jnp.float32
BF16 = jnp.bfloat16


def digit_sizes():
    rest = lax.axis_size("dp")
    core = 2 if rest % 2 == 0 else 1
    rest //= core
    across = 2 if rest % 2 == 0 else 1
    rest //= across
    return (rest, across, core, lax.axis_size("tensor"))


def my_digits(sizes):
    dp = lax.axis_index("dp")
    return (
        dp // (sizes[X] * sizes[C]),
        dp // sizes[C] % sizes[X],
        dp % sizes[C],
        lax.axis_index("tensor"),
    )


def hop(value, sizes, digit, step=1):
    pairs = []
    nz, nx, nc, ny = sizes
    for z in range(nz):
        for x in range(nx):
            for c in range(nc):
                for y in range(ny):
                    there = [z, x, c, y]
                    there[digit] = (there[digit] + step) % sizes[digit]
                    source = ((z * nx + x) * nc + c) * ny + y
                    target = ((there[0] * nx + there[1]) * nc + there[2]) * ny + there[3]
                    pairs.append((source, target))
    return lax.ppermute(value, ALL, pairs)


def ring(value, sizes, digit):
    pieces = [value]
    for _ in range(sizes[digit] - 1):
        pieces.append(hop(pieces[-1], sizes, digit))
    return pieces


def place(pieces, index, axis):
    count = len(pieces)
    if count == 1:
        return jnp.expand_dims(pieces[0], axis)
    shape = list(pieces[0].shape)
    shape.insert(axis, count)
    out = jnp.zeros(shape, pieces[0].dtype)
    for k, piece in enumerate(pieces):
        out = lax.dynamic_update_index_in_dim(out, piece, (index - k) % count, axis)
    return out


def pick(value, index, axis):
    return lax.dynamic_index_in_dim(value, index, axis, keepdims=False)


def spread_sum(value, sizes, digit, index, axis):
    count = sizes[digit]
    terms = [pick(value, index, axis)]
    for k in range(1, count):
        terms.append(hop(pick(value, (index + k) % count, axis), sizes, digit, k))
    return terms


def sum_over(value, sizes, digit, index, axis):
    return sum(spread_sum(value, sizes, digit, index, axis))


def sync(*values):
    return lax.optimization_barrier(values)


def all_sum(value, sizes, digit):
    return value + sum(hop(value, sizes, digit, k) for k in range(1, sizes[digit]))


def fan(value, sizes, digit):
    return [value] + [hop(value, sizes, digit, k) for k in range(1, sizes[digit])]


def arrange(pieces, shapes, moves, places):
    out = [jnp.zeros(shape, BF16) for shape in shapes]
    for source, low, width, target, begin, lead in moves:
        piece = pieces[source][..., low : low + width]
        start = [jnp.int32(0) if w is None else places[w].astype(jnp.int32) for w in lead]
        fixed = [n for n, w in enumerate(lead) if w is not None]
        piece = jnp.expand_dims(piece, fixed)
        start += [jnp.int32(0), jnp.int32(begin)]
        out[target] = lax.dynamic_update_slice(out[target], piece, start)
    return out


def gather_project(shard, sizes, at, later):
    half = shard.shape[1] // 2
    over_x = hop(shard[:, :half], sizes, X) if sizes[X] == 2 else None
    second = place(fan(shard[:, half:], sizes, Z), at[Z], 0)
    first = [shard[:, :half]] + ([over_x] if sizes[X] == 2 else [])
    first = fan(place(first, at[X], 0), sizes, Z)
    first, later = sync(first, later)
    first = place(first, at[Z], 0)
    second = place(fan(second, sizes, X), at[X], 1)
    both = jnp.concatenate([first, second], axis=-1)
    full = place(fan(both, sizes, C), at[C], 2)
    return full.reshape(-1, shard.shape[1]), later


def stack_z(pieces, sizes, at):
    depth, width = pieces[0].shape
    cut = (width // 2 + 127) // 128 * 128
    shapes = [(sizes[Z], depth, cut), (sizes[Z], depth, width - cut)]
    moves = []
    for k in range(sizes[Z]):
        moves.append((k, 0, cut, 0, 0, (k,)))
        moves.append((k, cut, width - cut, 1, 0, (k,)))
    return arrange(pieces, shapes, moves, [(at[Z] - k) % sizes[Z] for k in range(sizes[Z])])


def spread_sides(halves, sizes):
    over_x = [list(p) for p in zip(*[fan(b, sizes, X) for b in halves])]
    if sizes[X] == 2 and sizes[Y] == 2:
        return over_x, [hop(b, sizes, Y) for b in halves]
    return over_x, []


def spread_corner(over_x, over_y, sizes):
    if sizes[X] == 2 and sizes[Y] == 2:
        corner = [hop(over_x[1][0], sizes, Y), hop(over_y[1], sizes, X)]
        return [over_x, [over_y, corner]]
    both = [list(zip(*[fan(b, sizes, Y) for b in piece])) for piece in over_x]
    return [[both[j][k] for j in range(sizes[X])] for k in range(sizes[Y])]


def assemble(spreads, sizes, at, widths):
    begins = [sum(widths[:m]) for m in range(len(widths))]
    nz, depth, _ = spreads[0][0][0].shape
    pieces, moves, shapes = [], [], []
    for k, by_x in enumerate(spreads):
        shapes += [(nz, sizes[X], sizes[C], depth, width) for width in widths]
        for j, halves in enumerate(by_x):
            base = 0
            for half in halves:
                size = half.shape[-1]
                for c, part in enumerate(fan(half, sizes, C)):
                    for m, width in enumerate(widths):
                        low = max(begins[m], base)
                        high = min(begins[m] + width, base + size)
                        if low < high:
                            lead = (None, j, sizes[X] + c)
                            target = k * len(widths) + m
                            moves.append(
                                (len(pieces), low - base, high - low, target, low - begins[m], lead)
                            )
                    pieces.append(part)
                base += size
    places = [(at[X] - j) % sizes[X] for j in range(sizes[X])]
    places += [(at[C] - c) % sizes[C] for c in range(sizes[C])]
    mats = arrange(pieces, shapes, moves, places)
    mats = [m.reshape(-1, m.shape[-1]) for m in mats]
    count = len(widths)
    return [mats[k * count : (k + 1) * count] for k in range(len(spreads))]


def core_part(full, sizes, core):
    return pick(full.reshape(sizes[Z], sizes[X], sizes[C], -1, full.shape[-1]), core, 2)


def core_send(full, sizes, at):
    own = core_part(full, sizes, at[C])
    if sizes[C] == 1:
        return (own,)
    return (hop(core_part(full, sizes, (at[C] + 1) % sizes[C]), sizes, C), own)


def corner_step(parts, sizes, at):
    far_x = (at[X] + 1) % 2
    half = parts[0].shape[-1] // 2
    cut = lambda p, h: p[..., h * half : (h + 1) * half]
    own, over_x = pick(parts[0], at[X], 1), pick(parts[0], far_x, 1)
    over_y, corner = pick(parts[1], at[X], 1), pick(parts[1], far_x, 1)
    from_x = hop(cut(corner, 0), sizes, X)
    from_y = hop(cut(corner, 1), sizes, Y)
    return (own, over_x, over_y, from_x, from_y)


def side_step(held, sizes):
    own, over_x, over_y, from_x, from_y = held
    half = own.shape[-1] // 2
    cut = lambda p, h: p[..., h * half : (h + 1) * half]
    to_x = jnp.concatenate([cut(over_x, 0), cut(over_x, 1) + from_y], axis=-1)
    to_y = jnp.concatenate([cut(over_y, 0) + from_x, cut(over_y, 1)], axis=-1)
    return (own, hop(to_x, sizes, X), hop(to_y, sizes, Y))


def plain_square(parts, sizes, at):
    total = parts[0]
    for k in range(1, sizes[Y]):
        total = total + hop(parts[k], sizes, Y, -k)
    return (sum_over(total, sizes, X, at[X], 1),)


def norm_parts(rows):
    average = jnp.mean(rows, axis=-1, keepdims=True)
    centered = rows - average
    scale = lax.rsqrt(jnp.mean(centered * centered, axis=-1, keepdims=True) + EPS)
    return centered * scale, scale


def norm_back(grad, unit, scale, gain):
    inner = grad * gain
    return scale * (
        inner
        - jnp.mean(inner, axis=-1, keepdims=True)
        - unit * jnp.mean(inner * unit, axis=-1, keepdims=True)
    )


def gelu_both(upper):
    below = 0.5 + 0.5 * lax.erf(upper * 0.5**0.5)
    density = jnp.exp(-0.5 * upper * upper) * 0.3989422804014327
    return upper * below, below + upper * density


def dot(a, b, dims):
    return lax.dot_general(a, b, (dims, ((), ())), preferred_element_type=F32)


NN = ((1,), (0,))
NT = ((1,), (1,))
TN = ((0,), (0,))


def mm(a, b):
    return jnp.dot(a, b, preferred_element_type=F32)


def turn(block):
    return block.astype(F32).T.astype(BF16)


def half_of(block, head, axis):
    return jnp.where(
        lax.broadcasted_iota(jnp.int32, block.shape, axis) // HEAD_DIM == head, block, 0
    ).astype(block.dtype)


def set_bias(down_ref, along_ref, bias_ref):
    @pl.when(pl.program_id(0) == 0)
    def _():
        bias_ref[...] = jnp.where(down_ref[...] == along_ref[...], 0.0, BIG_NEGATIVE)


def attend_kernel(q_ref, k_ref, v_ref, down_ref, along_ref, low_ref, full_ref, log_ref, bias_ref):
    set_bias(down_ref, along_ref, bias_ref)
    rows = q_ref.shape[0]
    tile = min(TILE, rows)
    turned = turn(q_ref[...].astype(F32) * HEAD_DIM ** (-0.5))
    keys = [half_of(k_ref[...], i, 1) for i in range(2)]
    values = [half_of(v_ref[...], i, 1) for i in range(2)]
    for begin in range(0, rows, tile):
        cols = slice(begin, begin + tile)
        mixed = jnp.zeros((tile, PAIR), F32)
        for i in range(2):
            scores = mm(keys[i], turned[:, cols]) + bias_ref[:, cols]
            top = jnp.max(scores, axis=0, keepdims=True)
            weights = jnp.exp(scores - top)
            total = jnp.sum(weights, axis=0, keepdims=True)
            log_ref[0, i : i + 1, cols] = top + jnp.log(total)
            mixed += dot((weights * (1.0 / total)).astype(BF16), values[i], TN)
        full_ref[cols, :] = mixed
        low_ref[cols, :] = mixed.astype(BF16)


def attend_back_kernel(
    q_ref, k_ref, v_ref, down_ref, along_ref, full_ref, log_ref, grad_ref, out_ref, bias_ref
):
    set_bias(down_ref, along_ref, bias_ref)
    rows = q_ref.shape[0]
    tile = min(TILE, rows)
    query = (q_ref[...].astype(F32) * HEAD_DIM ** (-0.5)).astype(BF16)
    grad = grad_ref[...]
    turned, grad_turned, key_turned = turn(query), turn(grad), turn(k_ref[...])
    inner = (grad.astype(F32) * full_ref[...]).T
    key_grad = jnp.zeros((rows, PAIR), F32)
    value_grad = jnp.zeros((rows, PAIR), F32)
    query_grad = [jnp.zeros((PAIR, tile), F32) for _ in range(rows // tile)]
    for i in range(2):
        key, value = half_of(k_ref[...], i, 1), half_of(v_ref[...], i, 1)
        kept_query, kept_grad = half_of(query, i, 1), half_of(grad, i, 1)
        kept_key = half_of(key_turned, i, 0)
        delta = jnp.sum(inner[i * HEAD_DIM : (i + 1) * HEAD_DIM], axis=0, keepdims=True)
        for j in range(rows // tile):
            cols = slice(j * tile, (j + 1) * tile)
            scores = mm(key, turned[:, cols]) + bias_ref[:, cols]
            probs = jnp.exp(scores - log_ref[0, i : i + 1, cols])
            prob_grad = mm(value, grad_turned[:, cols])
            score_grad = (probs * (prob_grad - delta[:, cols])).astype(BF16)
            value_grad += mm(probs.astype(BF16), kept_grad[cols])
            key_grad += mm(score_grad, kept_query[cols])
            query_grad[j] += mm(kept_key, score_grad)
    for j in range(rows // tile):
        out_ref[0, j * tile : (j + 1) * tile, :] = (query_grad[j].T * HEAD_DIM ** (-0.5)).astype(
            BF16
        )
    out_ref[1] = key_grad.astype(BF16)
    out_ref[2] = value_grad.astype(BF16)


def third(begin):
    return lambda h: (0, begin + h)


def attention(projected, segment, first, count):
    rows, width = projected.shape
    pairs = width // 3 // PAIR
    block = lambda f: pl.BlockSpec((rows, PAIR), f)
    return pl.pallas_call(
        attend_kernel,
        grid=(count,),
        in_specs=[block(third(c * pairs + first)) for c in range(3)]
        + [
            pl.BlockSpec((rows, 1), lambda h: (0, 0)),
            pl.BlockSpec((1, rows), lambda h: (0, 0)),
        ],
        out_specs=[
            block(third(0)),
            block(third(0)),
            pl.BlockSpec((1, 2, rows), lambda h: (h, 0, 0)),
        ],
        out_shape=[
            jax.ShapeDtypeStruct((rows, count * PAIR), BF16),
            jax.ShapeDtypeStruct((rows, count * PAIR), F32),
            jax.ShapeDtypeStruct((count, 2, rows), F32),
        ],
        scratch_shapes=[pltpu.VMEM((rows, rows), F32)],
        compiler_params=pltpu.CompilerParams(vmem_limit_bytes=40 * 2**20),
        cost_estimate=pl.CostEstimate(
            flops=count * 16 * rows * rows * PAIR,
            bytes_accessed=16 * rows * count * PAIR,
            transcendentals=2 * count * rows * rows,
        ),
    )(projected, projected, projected, segment[:, None], segment[None, :])


def attention_back(projected, segment, full, logs, grad, first, count):
    rows, width = projected.shape
    pairs = width // 3 // PAIR
    block = lambda f: pl.BlockSpec((rows, PAIR), f)
    return pl.pallas_call(
        attend_back_kernel,
        grid=(count,),
        in_specs=[block(third(c * pairs + first)) for c in range(3)]
        + [
            pl.BlockSpec((rows, 1), lambda h: (0, 0)),
            pl.BlockSpec((1, rows), lambda h: (0, 0)),
            block(third(0)),
            pl.BlockSpec((1, 2, rows), lambda h: (h, 0, 0)),
            block(third(first)),
        ],
        out_specs=pl.BlockSpec((3, rows, PAIR), lambda h: (0, 0, h)),
        out_shape=jax.ShapeDtypeStruct((3, rows, count * PAIR), BF16),
        scratch_shapes=[pltpu.VMEM((rows, rows), F32)],
        compiler_params=pltpu.CompilerParams(vmem_limit_bytes=48 * 2**20),
        cost_estimate=pl.CostEstimate(
            flops=count * 40 * rows * rows * PAIR,
            bytes_accessed=20 * rows * count * PAIR,
            transcendentals=2 * count * rows * rows,
        ),
    )(projected, projected, projected, segment[:, None], segment[None, :], full, logs, grad)


def on_device(
    tokens,
    lengths,
    project_weight,
    project_bias,
    output_weight,
    output_bias,
    first_gain,
    first_shift,
    expand_weight,
    expand_bias,
    shrink_weight,
    shrink_bias,
    second_gain,
    second_shift,
    cotangent,
):
    sizes = digit_sizes()
    at = my_digits(sizes)
    n_t = sizes[Y]
    mine = at[Y]
    rows, width = tokens.shape
    all_rows = rows * n_t
    heads_width = project_weight.shape[2]
    hidden = expand_weight.shape[1]
    depth = project_weight.shape[1]
    pairs = heads_width // PAIR
    square = sizes[X] == 2 and n_t == 2

    ends = jnp.cumsum(lengths[0], dtype=jnp.int32)
    positions = lax.iota(jnp.int32, all_rows)
    segment = jnp.sum(
        (positions[:, None] >= ends[None, :]).astype(jnp.int32), axis=1, dtype=jnp.int32
    )
    valid = (mine * rows + lax.iota(jnp.int32, rows) < ends[-1])[:, None]

    calls = 2 if pairs % 2 == 0 else 1
    group = pairs // calls
    span = group * PAIR

    token_pieces = fan(tokens, sizes, Y)
    upper_shard = jnp.concatenate([output_weight.T, expand_weight], axis=1)
    proj, (upper_shard, token_pieces) = gather_project(
        jnp.transpose(project_weight, (1, 0, 2)).reshape(depth, 3 * heads_width),
        sizes,
        at,
        (upper_shard, token_pieces),
    )
    whole_tokens = place(token_pieces, mine, 0).reshape(all_rows, width)
    upper_z = fan(upper_shard, sizes, Z)
    expand_biases = fan(expand_bias, sizes, Y)

    bias = jnp.concatenate([project_bias[0], jnp.zeros_like(project_bias[0]), project_bias[1]])
    projected = (dot(whole_tokens, proj, NN) + bias).astype(BF16)
    projected, shrink_shard = sync(projected, shrink_weight.T)
    shrink_z = fan(shrink_shard, sizes, Z)
    fwd = [attention(projected, segment, 0, group)]
    fwd[0], upper_z, projected = sync(fwd[0], upper_z, projected)
    upper_x, upper_y = spread_sides(stack_z(upper_z, sizes, at), sizes)
    if calls == 2:
        fwd.append(attention(projected, segment, group, group))
    if square:
        fwd[-1], upper_x[1], upper_y, shrink_z = sync(fwd[-1], upper_x[1], upper_y, shrink_z)
    by_rows = jnp.concatenate([f[0] for f in fwd], axis=1).reshape(n_t, rows, heads_width)
    mixed = [pick(by_rows, mine, 0)]
    for k in range(1, n_t):
        mixed.append(hop(pick(by_rows, (mine + k) % n_t, 0), sizes, Y, k))

    upper_pieces = spread_corner(upper_x, upper_y, sizes)
    shrink_x, shrink_y = spread_sides(stack_z(shrink_z, sizes, at), sizes)
    if square:
        mixed, shrink_x[1][0], shrink_y[1] = sync(mixed, shrink_x[1][0], shrink_y[1])
    gathered = assemble(upper_pieces, sizes, at, (heads_width, hidden))
    mix = [g[0] for g in gathered]
    expand = [g[1] for g in gathered]
    attn = sum(dot(m, w, NT) for m, w in zip(mixed, mix)) + output_bias
    unit1, scale1 = norm_parts(tokens.astype(F32) + attn)
    normed1 = unit1 * first_gain + first_shift
    low1 = normed1.astype(BF16)
    active, slope = [], []
    for w, b in zip(expand, expand_biases):
        act, der = gelu_both(dot(low1, w, NN) + b)
        active.append(act.astype(BF16))
        slope.append(der.astype(BF16))
    shrink_pieces = spread_corner(shrink_x, shrink_y, sizes)
    shrink = [g[0] for g in assemble(shrink_pieces, sizes, at, (hidden,))]
    branch = sum(dot(a, w, NT) for a, w in zip(active, shrink)) + shrink_bias
    unit2, scale2 = norm_parts(normed1 + branch)
    layer_output = jnp.where(valid, unit2 * second_gain + second_shift, 0.0).astype(BF16)

    grad = jnp.where(valid, cotangent.astype(F32), 0.0)
    grad_second_gain = jnp.sum(grad * unit2, axis=0)
    grad_second_shift = jnp.sum(grad, axis=0)
    grad_r2 = norm_back(grad, unit2, scale2, second_gain)
    grad_branch = grad_r2.astype(BF16)
    grad_shrink_bias = jnp.sum(grad_branch, axis=0, dtype=F32)
    shrink_core = [core_send(dot(grad_branch, a, TN).astype(BF16), sizes, at) for a in active]
    grad_upper = [
        (dot(grad_branch, w, NN) * s.astype(F32)).astype(BF16) for w, s in zip(shrink, slope)
    ]
    grad_expand_biases = [jnp.sum(g, axis=0, dtype=F32) for g in grad_upper]
    grad_normed1 = sum(dot(g, w, NT) for g, w in zip(grad_upper, expand)) + grad_r2
    shrink_core, grad_normed1 = sync(shrink_core, grad_normed1)
    shrink_parts = [sum(parts) for parts in shrink_core]
    if square:
        shrink_held = corner_step(shrink_parts, sizes, at)
    grad_first_gain = jnp.sum(grad_normed1 * unit1, axis=0)
    grad_first_shift = jnp.sum(grad_normed1, axis=0)
    grad_r1 = norm_back(grad_normed1, unit1, scale1, first_gain)
    grad_attn = grad_r1.astype(BF16)
    grad_output_bias = jnp.sum(grad_attn, axis=0, dtype=F32)

    grad_pieces = []
    for k, w in enumerate(mix):
        part = dot(grad_attn, w, NN).astype(BF16)
        grad_pieces.append(hop(part, sizes, Y, -k) if k else part)
    low1, grad_attn = sync(low1, grad_attn)
    grad_expand = [dot(low1, g, TN).astype(BF16) for g in grad_upper]
    if square:
        grad_expand, shrink_held = sync(grad_expand, shrink_held)
        shrink_sides = side_step(shrink_held, sizes)
    else:
        shrink_sides = plain_square(shrink_parts, sizes, at)
    expand_core = [core_send(g, sizes, at) for g in grad_expand]
    grad_mix = [dot(grad_attn, m, TN).astype(BF16) for m in mixed]
    mix_core = [core_send(g, sizes, at) for g in grad_mix]
    grad_rows = place([grad_pieces[-k % n_t] for k in range(n_t)], mine, 0)
    grad_rows = grad_rows.reshape(all_rows, heads_width)
    packed = jnp.concatenate(
        [
            grad_second_gain,
            grad_second_shift,
            grad_shrink_bias,
            grad_first_gain,
            grad_first_shift,
            grad_output_bias,
            place(grad_expand_biases, mine, 0).reshape(-1),
        ]
    )
    grad_rows, mix_core, expand_core, packed = sync(grad_rows, mix_core, expand_core, packed)
    upper_parts = [
        jnp.concatenate([sum(a), sum(b)], axis=-1) for a, b in zip(mix_core, expand_core)
    ]
    if square:
        upper_held = corner_step(upper_parts, sizes, at)
    else:
        upper_sides = plain_square(upper_parts, sizes, at)
    packed = all_sum(packed, sizes, C)

    back = []
    project_sums = []
    bias_sums = []
    for n in range(calls):
        low, full, logs = fwd[n]
        part = attention_back(projected, segment, full, logs, grad_rows, n * group, group)
        if n == 0:
            if square:
                part, shrink_sides, upper_held, packed, grad_rows = sync(
                    part, shrink_sides, upper_held, packed, grad_rows
                )
                upper_sides = side_step(upper_held, sizes)
            shrink_z = spread_sum(sum(shrink_sides), sizes, Z, at[Z], 0)
            packed = all_sum(packed, sizes, X)
        back.append(part)
        columns = jnp.concatenate([part[c] for c in range(3)], axis=-1)
        bias_sums.append(jnp.sum(columns, axis=0, dtype=F32))
        project_sums.append(core_send(dot(whole_tokens, columns, TN).astype(BF16), sizes, at))
        if n == 0:
            project_sums[0], grad_rows = sync(project_sums[0], grad_rows)
            project_x = [spread_sum(sum(project_sums[0]), sizes, X, at[X], 1)]
    projected_grad = jnp.concatenate([b[c] for c in range(3) for b in back], axis=-1)
    bias_sum = jnp.concatenate([b.reshape(3, span) for b in bias_sums], axis=-1)
    bias_sum = jnp.stack([bias_sum[0], bias_sum[2]]).reshape(-1)
    bias_sum = all_sum(bias_sum, sizes, C)
    token_parts = []
    for k in range(n_t):
        begin = (mine + k) % n_t * rows
        part = dot(lax.dynamic_slice_in_dim(projected_grad, begin, rows, 0), proj, NT)
        token_parts.append(part.astype(BF16) if k else part)
    project_sums, project_x, upper_sides, shrink_z, token_parts, packed, bias_sum = sync(
        project_sums, project_x, upper_sides, shrink_z, token_parts, packed, bias_sum
    )
    token_parts = [hop(p, sizes, Y, k) if k else p for k, p in enumerate(token_parts)]
    packed = all_sum(packed, sizes, Y)
    bias_sum = all_sum(bias_sum, sizes, X)
    grad_shrink_weight = sum(shrink_z).astype(F32).T
    owned_upper = spread_sum(sum(upper_sides), sizes, Z, at[Z], 0)
    owned = [spread_sum(sum(project_x[0]), sizes, Z, at[Z], 0)]
    for parts in project_sums[1:]:
        total = sum_over(sum(parts), sizes, X, at[X], 1)
        total, owned_upper, owned[0], token_parts, packed, bias_sum = sync(
            total, owned_upper, owned[0], token_parts, packed, bias_sum
        )
        owned.append(spread_sum(total, sizes, Z, at[Z], 0))
    owned = [sum(o).reshape(depth, 3, span) for o in owned]
    grad_project_weight = jnp.transpose(
        jnp.concatenate(owned, axis=-1), (1, 0, 2)
    ).astype(F32)
    owned = sum(owned_upper).astype(F32)
    grad_output_weight = owned[:, :heads_width].T
    grad_expand_weight = owned[:, heads_width:]

    packed = all_sum(jnp.concatenate([packed, bias_sum]), sizes, Z)
    grad_project_bias = packed[-bias_sum.shape[0] :].reshape(2, heads_width)
    packed = packed[: -bias_sum.shape[0]]
    (
        grad_second_gain,
        grad_second_shift,
        grad_shrink_bias,
        grad_first_gain,
        grad_first_shift,
        grad_output_bias,
    ) = (packed[i * width : (i + 1) * width] for i in range(6))
    grad_expand_bias = pick(packed[6 * width :].reshape(n_t, hidden), mine, 0)
    grad_tokens = (grad_r1 + sum(p.astype(F32) for p in token_parts)).astype(BF16)
    return (
        layer_output,
        grad_tokens,
        grad_project_weight,
        grad_project_bias,
        grad_output_weight,
        grad_output_bias,
        grad_first_gain,
        grad_first_shift,
        grad_expand_weight,
        grad_expand_bias,
        grad_shrink_weight,
        grad_shrink_bias,
        grad_second_gain,
        grad_second_shift,
    )


def solution(mesh):
    rows = P(("dp", "tensor"), None)
    weights = (P(None, "dp", "tensor"), P("tensor", "dp"), P("dp", "tensor"), P("tensor", "dp"))
    in_specs = (
        rows,
        P("dp", None),
        weights[0],
        P(None, "tensor"),
        weights[1],
        P(),
        P(),
        P(),
        weights[2],
        P("tensor"),
        weights[3],
        P(),
        P(),
        P(),
        rows,
    )
    out_specs = (
        rows,
        rows,
        weights[0],
        P(None, "tensor"),
        weights[1],
        P(),
        P(),
        P(),
        weights[2],
        P("tensor"),
        weights[3],
        P(),
        P(),
        P(),
    )
    return jax.shard_map(
        on_device, mesh=mesh, in_specs=in_specs, out_specs=out_specs, check_vma=False
    )
```

```python
import jax
import jax.numpy as jnp
from jax import lax
from jax.experimental import pallas as pl
from jax.experimental.pallas import tpu as pltpu
from jax.sharding import PartitionSpec as P

HEAD_DIM = 64
TILE = 256
PAIR = 2 * HEAD_DIM
EPS = 1e-05
BIG_NEGATIVE = -1e30
ALL = ("dp", "tensor")
Z, X, C, Y = range(4)
F32 = jnp.float32
BF16 = jnp.bfloat16


def digit_sizes():
    rest = lax.axis_size("dp")
    core = 2 if rest % 2 == 0 else 1
    rest //= core
    across = 2 if rest % 2 == 0 else 1
    rest //= across
    return (rest, across, core, lax.axis_size("tensor"))


def my_digits(sizes):
    dp = lax.axis_index("dp")
    return (
        dp // (sizes[X] * sizes[C]),
        dp // sizes[C] % sizes[X],
        dp % sizes[C],
        lax.axis_index("tensor"),
    )


def hop(value, sizes, digit, step=1):
    pairs = []
    nz, nx, nc, ny = sizes
    for z in range(nz):
        for x in range(nx):
            for c in range(nc):
                for y in range(ny):
                    there = [z, x, c, y]
                    there[digit] = (there[digit] + step) % sizes[digit]
                    source = ((z * nx + x) * nc + c) * ny + y
                    target = ((there[0] * nx + there[1]) * nc + there[2]) * ny + there[3]
                    pairs.append((source, target))
    return lax.ppermute(value, ALL, pairs)


def ring(value, sizes, digit):
    pieces = [value]
    for _ in range(sizes[digit] - 1):
        pieces.append(hop(pieces[-1], sizes, digit))
    return pieces


def place(pieces, index, axis):
    count = len(pieces)
    if count == 1:
        return jnp.expand_dims(pieces[0], axis)
    shape = list(pieces[0].shape)
    shape.insert(axis, count)
    out = jnp.zeros(shape, pieces[0].dtype)
    for k, piece in enumerate(pieces):
        out = lax.dynamic_update_index_in_dim(out, piece, (index - k) % count, axis)
    return out


def pick(value, index, axis):
    return lax.dynamic_index_in_dim(value, index, axis, keepdims=False)


def spread_sum(value, sizes, digit, index, axis):
    count = sizes[digit]
    terms = [pick(value, index, axis)]
    for k in range(1, count):
        terms.append(hop(pick(value, (index + k) % count, axis), sizes, digit, k))
    return terms


def sum_over(value, sizes, digit, index, axis):
    return sum(spread_sum(value, sizes, digit, index, axis))


def sync(*values):
    return lax.optimization_barrier(values)


def all_sum(value, sizes, digit):
    return value + sum(hop(value, sizes, digit, k) for k in range(1, sizes[digit]))


def fan(value, sizes, digit):
    return [value] + [hop(value, sizes, digit, k) for k in range(1, sizes[digit])]


def arrange(pieces, shapes, moves, places):
    out = [jnp.zeros(shape, BF16) for shape in shapes]
    for source, low, width, target, begin, lead in moves:
        piece = pieces[source][..., low : low + width]
        start = [jnp.int32(0) if w is None else places[w].astype(jnp.int32) for w in lead]
        fixed = [n for n, w in enumerate(lead) if w is not None]
        piece = jnp.expand_dims(piece, fixed)
        start += [jnp.int32(0), jnp.int32(begin)]
        out[target] = lax.dynamic_update_slice(out[target], piece, start)
    return out


def gather_project(shard, sizes, at, later):
    half = shard.shape[1] // 2
    over_x = hop(shard[:, :half], sizes, X) if sizes[X] == 2 else None
    second = place(fan(shard[:, half:], sizes, Z), at[Z], 0)
    first = [shard[:, :half]] + ([over_x] if sizes[X] == 2 else [])
    first = fan(place(first, at[X], 0), sizes, Z)
    first, later = sync(first, later)
    first = place(first, at[Z], 0)
    second = place(fan(second, sizes, X), at[X], 1)
    both = jnp.concatenate([first, second], axis=-1)
    full = place(fan(both, sizes, C), at[C], 2)
    return full.reshape(-1, shard.shape[1]), later


def stack_z(pieces, sizes, at):
    depth, width = pieces[0].shape
    cut = (width // 2 + 127) // 128 * 128
    shapes = [(sizes[Z], depth, cut), (sizes[Z], depth, width - cut)]
    moves = []
    for k in range(sizes[Z]):
        moves.append((k, 0, cut, 0, 0, (k,)))
        moves.append((k, cut, width - cut, 1, 0, (k,)))
    return arrange(pieces, shapes, moves, [(at[Z] - k) % sizes[Z] for k in range(sizes[Z])])


def spread_sides(halves, sizes):
    over_x = [list(p) for p in zip(*[fan(b, sizes, X) for b in halves])]
    if sizes[X] == 2 and sizes[Y] == 2:
        return over_x, [hop(b, sizes, Y) for b in halves]
    return over_x, []


def spread_corner(over_x, over_y, sizes):
    if sizes[X] == 2 and sizes[Y] == 2:
        corner = [hop(over_x[1][0], sizes, Y), hop(over_y[1], sizes, X)]
        return [over_x, [over_y, corner]]
    both = [list(zip(*[fan(b, sizes, Y) for b in piece])) for piece in over_x]
    return [[both[j][k] for j in range(sizes[X])] for k in range(sizes[Y])]


def last_digit(stacked, sizes, digit):
    count = stacked.shape[1]
    cored = [fan(piece, sizes, C) for piece in fan(stacked, sizes, digit)]
    return [[[part[:, n] for part in by_core] for n in range(count)] for by_core in cored]


def assemble(spreads, sizes, at, widths):
    begins = [sum(widths[:m]) for m in range(len(widths))]
    nz, depth, _ = spreads[0][0][0][0].shape
    pieces, moves, shapes = [], [], []
    for k, by_x in enumerate(spreads):
        shapes += [(nz, sizes[X], sizes[C], depth, width) for width in widths]
        for j, halves in enumerate(by_x):
            base = 0
            for half in halves:
                size = half[0].shape[-1]
                for c, part in enumerate(half):
                    for m, width in enumerate(widths):
                        low = max(begins[m], base)
                        high = min(begins[m] + width, base + size)
                        if low < high:
                            lead = (None, j, sizes[X] + c)
                            target = k * len(widths) + m
                            moves.append(
                                (len(pieces), low - base, high - low, target, low - begins[m], lead)
                            )
                    pieces.append(part)
                base += size
    places = [(at[X] - j) % sizes[X] for j in range(sizes[X])]
    places += [(at[C] - c) % sizes[C] for c in range(sizes[C])]
    mats = arrange(pieces, shapes, moves, places)
    mats = [m.reshape(-1, m.shape[-1]) for m in mats]
    count = len(widths)
    return [mats[k * count : (k + 1) * count] for k in range(len(spreads))]


def core_part(full, sizes, core):
    return pick(full.reshape(sizes[Z], sizes[X], sizes[C], -1, full.shape[-1]), core, 2)


def core_send(full, sizes, at):
    own = core_part(full, sizes, at[C])
    if sizes[C] == 1:
        return (own,)
    return (hop(core_part(full, sizes, (at[C] + 1) % sizes[C]), sizes, C), own)


def corner_step(parts, sizes, at):
    far_x = (at[X] + 1) % 2
    half = parts[0].shape[-1] // 2
    cut = lambda p, h: p[..., h * half : (h + 1) * half]
    own, over_x = pick(parts[0], at[X], 1), pick(parts[0], far_x, 1)
    over_y, corner = pick(parts[1], at[X], 1), pick(parts[1], far_x, 1)
    from_x = hop(cut(corner, 0), sizes, X)
    from_y = hop(cut(corner, 1), sizes, Y)
    return (own, over_x, over_y, from_x, from_y)


def side_step(held, sizes):
    own, over_x, over_y, from_x, from_y = held
    half = own.shape[-1] // 2
    cut = lambda p, h: p[..., h * half : (h + 1) * half]
    to_x = jnp.concatenate([cut(over_x, 0), cut(over_x, 1) + from_y], axis=-1)
    to_y = jnp.concatenate([cut(over_y, 0) + from_x, cut(over_y, 1)], axis=-1)
    return (own, hop(to_x, sizes, X), hop(to_y, sizes, Y))


def plain_square(parts, sizes, at):
    total = parts[0]
    for k in range(1, sizes[Y]):
        total = total + hop(parts[k], sizes, Y, -k)
    return (sum_over(total, sizes, X, at[X], 1),)


def norm_parts(rows):
    average = jnp.mean(rows, axis=-1, keepdims=True)
    centered = rows - average
    scale = lax.rsqrt(jnp.mean(centered * centered, axis=-1, keepdims=True) + EPS)
    return centered * scale, scale


def norm_back(grad, unit, scale, gain):
    inner = grad * gain
    return scale * (
        inner
        - jnp.mean(inner, axis=-1, keepdims=True)
        - unit * jnp.mean(inner * unit, axis=-1, keepdims=True)
    )


def gelu_both(upper):
    below = 0.5 + 0.5 * lax.erf(upper * 0.5**0.5)
    density = jnp.exp(-0.5 * upper * upper) * 0.3989422804014327
    return upper * below, below + upper * density


def dot(a, b, dims):
    return lax.dot_general(a, b, (dims, ((), ())), preferred_element_type=F32)


NN = ((1,), (0,))
NT = ((1,), (1,))
TN = ((0,), (0,))


def mm(a, b):
    return jnp.dot(a, b, preferred_element_type=F32)


def turn(block):
    return block.astype(F32).T.astype(BF16)


def half_of(block, head, axis):
    return jnp.where(
        lax.broadcasted_iota(jnp.int32, block.shape, axis) // HEAD_DIM == head, block, 0
    ).astype(block.dtype)


def set_bias(down_ref, along_ref, bias_ref):
    @pl.when(pl.program_id(0) == 0)
    def _():
        bias_ref[...] = jnp.where(down_ref[...] == along_ref[...], 0.0, BIG_NEGATIVE)


def attend_kernel(q_ref, k_ref, v_ref, down_ref, along_ref, low_ref, full_ref, log_ref, bias_ref):
    set_bias(down_ref, along_ref, bias_ref)
    rows = q_ref.shape[0]
    tile = min(TILE, rows)
    turned = turn(q_ref[...].astype(F32) * HEAD_DIM ** (-0.5))
    keys = [half_of(k_ref[...], i, 1) for i in range(2)]
    values = [half_of(v_ref[...], i, 1) for i in range(2)]
    for begin in range(0, rows, tile):
        cols = slice(begin, begin + tile)
        mixed = jnp.zeros((tile, PAIR), F32)
        for i in range(2):
            scores = mm(keys[i], turned[:, cols]) + bias_ref[:, cols]
            top = jnp.max(scores, axis=0, keepdims=True)
            weights = jnp.exp(scores - top)
            total = jnp.sum(weights, axis=0, keepdims=True)
            log_ref[0, i : i + 1, cols] = top + jnp.log(total)
            mixed += dot((weights * (1.0 / total)).astype(BF16), values[i], TN)
        full_ref[cols, :] = mixed
        low_ref[cols, :] = mixed.astype(BF16)


def attend_back_kernel(
    q_ref, k_ref, v_ref, down_ref, along_ref, full_ref, log_ref, grad_ref, out_ref, bias_ref
):
    set_bias(down_ref, along_ref, bias_ref)
    rows = q_ref.shape[0]
    tile = min(TILE, rows)
    query = (q_ref[...].astype(F32) * HEAD_DIM ** (-0.5)).astype(BF16)
    grad = grad_ref[...]
    turned, grad_turned, key_turned = turn(query), turn(grad), turn(k_ref[...])
    inner = (grad.astype(F32) * full_ref[...]).T
    key_grad = jnp.zeros((rows, PAIR), F32)
    value_grad = jnp.zeros((rows, PAIR), F32)
    query_grad = [jnp.zeros((PAIR, tile), F32) for _ in range(rows // tile)]
    for i in range(2):
        key, value = half_of(k_ref[...], i, 1), half_of(v_ref[...], i, 1)
        kept_query, kept_grad = half_of(query, i, 1), half_of(grad, i, 1)
        kept_key = half_of(key_turned, i, 0)
        delta = jnp.sum(inner[i * HEAD_DIM : (i + 1) * HEAD_DIM], axis=0, keepdims=True)
        for j in range(rows // tile):
            cols = slice(j * tile, (j + 1) * tile)
            scores = mm(key, turned[:, cols]) + bias_ref[:, cols]
            probs = jnp.exp(scores - log_ref[0, i : i + 1, cols])
            prob_grad = mm(value, grad_turned[:, cols])
            score_grad = (probs * (prob_grad - delta[:, cols])).astype(BF16)
            value_grad += mm(probs.astype(BF16), kept_grad[cols])
            key_grad += mm(score_grad, kept_query[cols])
            query_grad[j] += mm(kept_key, score_grad)
    for j in range(rows // tile):
        out_ref[0, j * tile : (j + 1) * tile, :] = (query_grad[j].T * HEAD_DIM ** (-0.5)).astype(
            BF16
        )
    out_ref[1] = key_grad.astype(BF16)
    out_ref[2] = value_grad.astype(BF16)


def third(begin):
    return lambda h: (0, begin + h)


def attention(projected, segment, first, count):
    rows, width = projected.shape
    pairs = width // 3 // PAIR
    block = lambda f: pl.BlockSpec((rows, PAIR), f)
    return pl.pallas_call(
        attend_kernel,
        grid=(count,),
        in_specs=[block(third(c * pairs + first)) for c in range(3)]
        + [
            pl.BlockSpec((rows, 1), lambda h: (0, 0)),
            pl.BlockSpec((1, rows), lambda h: (0, 0)),
        ],
        out_specs=[
            block(third(0)),
            block(third(0)),
            pl.BlockSpec((1, 2, rows), lambda h: (h, 0, 0)),
        ],
        out_shape=[
            jax.ShapeDtypeStruct((rows, count * PAIR), BF16),
            jax.ShapeDtypeStruct((rows, count * PAIR), F32),
            jax.ShapeDtypeStruct((count, 2, rows), F32),
        ],
        scratch_shapes=[pltpu.VMEM((rows, rows), F32)],
        compiler_params=pltpu.CompilerParams(vmem_limit_bytes=40 * 2**20),
        cost_estimate=pl.CostEstimate(
            flops=count * 16 * rows * rows * PAIR,
            bytes_accessed=16 * rows * count * PAIR,
            transcendentals=2 * count * rows * rows,
        ),
    )(projected, projected, projected, segment[:, None], segment[None, :])


def attention_back(projected, segment, full, logs, grad, first, count):
    rows, width = projected.shape
    pairs = width // 3 // PAIR
    block = lambda f: pl.BlockSpec((rows, PAIR), f)
    return pl.pallas_call(
        attend_back_kernel,
        grid=(count,),
        in_specs=[block(third(c * pairs + first)) for c in range(3)]
        + [
            pl.BlockSpec((rows, 1), lambda h: (0, 0)),
            pl.BlockSpec((1, rows), lambda h: (0, 0)),
            block(third(0)),
            pl.BlockSpec((1, 2, rows), lambda h: (h, 0, 0)),
            block(third(first)),
        ],
        out_specs=pl.BlockSpec((3, rows, PAIR), lambda h: (0, 0, h)),
        out_shape=jax.ShapeDtypeStruct((3, rows, count * PAIR), BF16),
        scratch_shapes=[pltpu.VMEM((rows, rows), F32)],
        compiler_params=pltpu.CompilerParams(vmem_limit_bytes=48 * 2**20),
        cost_estimate=pl.CostEstimate(
            flops=count * 40 * rows * rows * PAIR,
            bytes_accessed=20 * rows * count * PAIR,
            transcendentals=2 * count * rows * rows,
        ),
    )(projected, projected, projected, segment[:, None], segment[None, :], full, logs, grad)


def on_device(
    tokens,
    lengths,
    project_weight,
    project_bias,
    output_weight,
    output_bias,
    first_gain,
    first_shift,
    expand_weight,
    expand_bias,
    shrink_weight,
    shrink_bias,
    second_gain,
    second_shift,
    cotangent,
):
    sizes = digit_sizes()
    at = my_digits(sizes)
    n_t = sizes[Y]
    mine = at[Y]
    rows, width = tokens.shape
    all_rows = rows * n_t
    heads_width = project_weight.shape[2]
    hidden = expand_weight.shape[1]
    depth = project_weight.shape[1]
    pairs = heads_width // PAIR
    square = sizes[X] == 2 and n_t == 2

    ends = jnp.cumsum(lengths[0], dtype=jnp.int32)
    positions = lax.iota(jnp.int32, all_rows)
    segment = jnp.sum(
        (positions[:, None] >= ends[None, :]).astype(jnp.int32), axis=1, dtype=jnp.int32
    )
    valid = (mine * rows + lax.iota(jnp.int32, rows) < ends[-1])[:, None]

    calls = 2 if pairs % 2 == 0 else 1
    group = pairs // calls
    span = group * PAIR

    token_pieces = fan(tokens, sizes, Y)
    upper_shard = jnp.concatenate([output_weight.T, expand_weight], axis=1)
    proj, (upper_shard, token_pieces, shrink_shard) = gather_project(
        jnp.transpose(project_weight, (1, 0, 2)).reshape(depth, 3 * heads_width),
        sizes,
        at,
        (upper_shard, token_pieces, shrink_weight.T),
    )
    whole_tokens = place(token_pieces, mine, 0).reshape(all_rows, width)
    upper_z = fan(upper_shard, sizes, Z)
    cut = hidden // 2
    shrink_y = jnp.stack(fan(shrink_shard[:, :cut], sizes, Y))
    shrink_x = jnp.stack(fan(shrink_shard[:, cut:], sizes, X))
    expand_biases = fan(expand_bias, sizes, Y)

    bias = jnp.concatenate([project_bias[0], jnp.zeros_like(project_bias[0]), project_bias[1]])
    projected = (dot(whole_tokens, proj, NN) + bias).astype(BF16)
    projected, shrink_y, shrink_x = sync(projected, shrink_y, shrink_x)
    shrink_y = fan(shrink_y, sizes, Z)
    fwd = [attention(projected, segment, 0, group)]
    fwd[0], upper_z, projected = sync(fwd[0], upper_z, projected)
    upper_x, upper_y = spread_sides(stack_z(upper_z, sizes, at), sizes)
    if calls == 2:
        fwd.append(attention(projected, segment, group, group))
    if square:
        fwd[-1], upper_x[1], upper_y, shrink_y = sync(fwd[-1], upper_x[1], upper_y, shrink_y)
    by_rows = jnp.concatenate([f[0] for f in fwd], axis=1).reshape(n_t, rows, heads_width)
    mixed = [pick(by_rows, mine, 0)]
    for k in range(1, n_t):
        mixed.append(hop(pick(by_rows, (mine + k) % n_t, 0), sizes, Y, k))

    upper_pieces = spread_corner(upper_x, upper_y, sizes)
    shrink_x = fan(shrink_x, sizes, Z)
    mixed, shrink_x = sync(mixed, shrink_x)
    over_x = last_digit(place(shrink_y, at[Z], 0), sizes, X)
    over_y = last_digit(place(shrink_x, at[Z], 0), sizes, Y)
    upper_pieces = [[[fan(h, sizes, C) for h in by_h] for by_h in by_x] for by_x in upper_pieces]
    gathered = assemble(upper_pieces, sizes, at, (heads_width, hidden))
    mix = [g[0] for g in gathered]
    expand = [g[1] for g in gathered]
    attn = sum(dot(m, w, NT) for m, w in zip(mixed, mix)) + output_bias
    unit1, scale1 = norm_parts(tokens.astype(F32) + attn)
    normed1 = unit1 * first_gain + first_shift
    low1 = normed1.astype(BF16)
    active, slope = [], []
    for w, b in zip(expand, expand_biases):
        act, der = gelu_both(dot(low1, w, NN) + b)
        active.append(act.astype(BF16))
        slope.append(der.astype(BF16))
    shrink_pieces = [
        [[over_x[j][k], over_y[k][j]] for j in range(sizes[X])] for k in range(n_t)
    ]
    shrink = [g[0] for g in assemble(shrink_pieces, sizes, at, (hidden,))]
    branch = sum(dot(a, w, NT) for a, w in zip(active, shrink)) + shrink_bias
    unit2, scale2 = norm_parts(normed1 + branch)
    layer_output = jnp.where(valid, unit2 * second_gain + second_shift, 0.0).astype(BF16)

    grad = jnp.where(valid, cotangent.astype(F32), 0.0)
    grad_second_gain = jnp.sum(grad * unit2, axis=0)
    grad_second_shift = jnp.sum(grad, axis=0)
    grad_r2 = norm_back(grad, unit2, scale2, second_gain)
    grad_branch = grad_r2.astype(BF16)
    grad_shrink_bias = jnp.sum(grad_branch, axis=0, dtype=F32)
    shrink_core = [core_send(dot(grad_branch, a, TN).astype(BF16), sizes, at) for a in active]
    grad_upper = [
        (dot(grad_branch, w, NN) * s.astype(F32)).astype(BF16) for w, s in zip(shrink, slope)
    ]
    grad_expand_biases = [jnp.sum(g, axis=0, dtype=F32) for g in grad_upper]
    grad_normed1 = sum(dot(g, w, NT) for g, w in zip(grad_upper, expand)) + grad_r2
    shrink_core, grad_normed1 = sync(shrink_core, grad_normed1)
    shrink_parts = [sum(parts) for parts in shrink_core]
    if square:
        shrink_held = corner_step(shrink_parts, sizes, at)
    grad_first_gain = jnp.sum(grad_normed1 * unit1, axis=0)
    grad_first_shift = jnp.sum(grad_normed1, axis=0)
    grad_r1 = norm_back(grad_normed1, unit1, scale1, first_gain)
    grad_attn = grad_r1.astype(BF16)
    grad_output_bias = jnp.sum(grad_attn, axis=0, dtype=F32)

    grad_pieces = []
    for k, w in enumerate(mix):
        part = dot(grad_attn, w, NN).astype(BF16)
        grad_pieces.append(hop(part, sizes, Y, -k) if k else part)
    low1, grad_attn = sync(low1, grad_attn)
    grad_expand = [dot(low1, g, TN).astype(BF16) for g in grad_upper]
    if square:
        grad_expand, shrink_held = sync(grad_expand, shrink_held)
        shrink_sides = side_step(shrink_held, sizes)
    else:
        shrink_sides = plain_square(shrink_parts, sizes, at)
    expand_core = [core_send(g, sizes, at) for g in grad_expand]
    grad_mix = [dot(grad_attn, m, TN).astype(BF16) for m in mixed]
    mix_core = [core_send(g, sizes, at) for g in grad_mix]
    grad_rows = place([grad_pieces[-k % n_t] for k in range(n_t)], mine, 0)
    grad_rows = grad_rows.reshape(all_rows, heads_width)
    packed = jnp.concatenate(
        [
            grad_second_gain,
            grad_second_shift,
            grad_shrink_bias,
            grad_first_gain,
            grad_first_shift,
            grad_output_bias,
            place(grad_expand_biases, mine, 0).reshape(-1),
        ]
    )
    grad_rows, mix_core, expand_core, packed = sync(grad_rows, mix_core, expand_core, packed)
    upper_parts = [
        jnp.concatenate([sum(a), sum(b)], axis=-1) for a, b in zip(mix_core, expand_core)
    ]
    if square:
        upper_held = corner_step(upper_parts, sizes, at)
    else:
        upper_sides = plain_square(upper_parts, sizes, at)
    packed = all_sum(packed, sizes, C)

    back = []
    project_sums = []
    bias_sums = []
    for n in range(calls):
        low, full, logs = fwd[n]
        part = attention_back(projected, segment, full, logs, grad_rows, n * group, group)
        if n == 0:
            if square:
                part, shrink_sides, upper_held, packed, grad_rows = sync(
                    part, shrink_sides, upper_held, packed, grad_rows
                )
                upper_sides = side_step(upper_held, sizes)
            shrink_z = spread_sum(sum(shrink_sides), sizes, Z, at[Z], 0)
            packed = all_sum(packed, sizes, X)
        back.append(part)
        columns = jnp.concatenate([part[c] for c in range(3)], axis=-1)
        bias_sums.append(jnp.sum(columns, axis=0, dtype=F32))
        project_sums.append(core_send(dot(whole_tokens, columns, TN).astype(BF16), sizes, at))
        if n == 0:
            project_sums[0], grad_rows = sync(project_sums[0], grad_rows)
            project_x = [spread_sum(sum(project_sums[0]), sizes, X, at[X], 1)]
    projected_grad = jnp.concatenate([b[c] for c in range(3) for b in back], axis=-1)
    bias_sum = jnp.concatenate([b.reshape(3, span) for b in bias_sums], axis=-1)
    bias_sum = jnp.stack([bias_sum[0], bias_sum[2]]).reshape(-1)
    bias_sum = all_sum(bias_sum, sizes, C)
    token_parts = []
    for k in range(n_t):
        begin = (mine + k) % n_t * rows
        part = dot(lax.dynamic_slice_in_dim(projected_grad, begin, rows, 0), proj, NT)
        token_parts.append(part.astype(BF16) if k else part)
    project_sums, project_x, upper_sides, shrink_z, token_parts, packed, bias_sum = sync(
        project_sums, project_x, upper_sides, shrink_z, token_parts, packed, bias_sum
    )
    token_parts = [hop(p, sizes, Y, k) if k else p for k, p in enumerate(token_parts)]
    packed = all_sum(packed, sizes, Y)
    bias_sum = all_sum(bias_sum, sizes, X)
    grad_shrink_weight = sum(shrink_z).astype(F32).T
    owned_upper = spread_sum(sum(upper_sides), sizes, Z, at[Z], 0)
    owned = [spread_sum(sum(project_x[0]), sizes, Z, at[Z], 0)]
    for parts in project_sums[1:]:
        total = sum_over(sum(parts), sizes, X, at[X], 1)
        total, owned_upper, owned[0], token_parts, packed, bias_sum = sync(
            total, owned_upper, owned[0], token_parts, packed, bias_sum
        )
        owned.append(spread_sum(total, sizes, Z, at[Z], 0))
    owned = [sum(o).reshape(depth, 3, span) for o in owned]
    grad_project_weight = jnp.transpose(
        jnp.concatenate(owned, axis=-1), (1, 0, 2)
    ).astype(F32)
    owned = sum(owned_upper).astype(F32)
    grad_output_weight = owned[:, :heads_width].T
    grad_expand_weight = owned[:, heads_width:]

    packed = all_sum(jnp.concatenate([packed, bias_sum]), sizes, Z)
    grad_project_bias = packed[-bias_sum.shape[0] :].reshape(2, heads_width)
    packed = packed[: -bias_sum.shape[0]]
    (
        grad_second_gain,
        grad_second_shift,
        grad_shrink_bias,
        grad_first_gain,
        grad_first_shift,
        grad_output_bias,
    ) = (packed[i * width : (i + 1) * width] for i in range(6))
    grad_expand_bias = pick(packed[6 * width :].reshape(n_t, hidden), mine, 0)
    grad_tokens = (grad_r1 + sum(p.astype(F32) for p in token_parts)).astype(BF16)
    return (
        layer_output,
        grad_tokens,
        grad_project_weight,
        grad_project_bias,
        grad_output_weight,
        grad_output_bias,
        grad_first_gain,
        grad_first_shift,
        grad_expand_weight,
        grad_expand_bias,
        grad_shrink_weight,
        grad_shrink_bias,
        grad_second_gain,
        grad_second_shift,
    )


def solution(mesh):
    rows = P(("dp", "tensor"), None)
    weights = (P(None, "dp", "tensor"), P("tensor", "dp"), P("dp", "tensor"), P("tensor", "dp"))
    in_specs = (
        rows,
        P("dp", None),
        weights[0],
        P(None, "tensor"),
        weights[1],
        P(),
        P(),
        P(),
        weights[2],
        P("tensor"),
        weights[3],
        P(),
        P(),
        P(),
        rows,
    )
    out_specs = (
        rows,
        rows,
        weights[0],
        P(None, "tensor"),
        weights[1],
        P(),
        P(),
        P(),
        weights[2],
        P("tensor"),
        weights[3],
        P(),
        P(),
        P(),
    )
    return jax.shard_map(
        on_device, mesh=mesh, in_specs=in_specs, out_specs=out_specs, check_vma=False
    )
```
